512 devices in a mesh: dp: 64 (over z, x), tensor: 8 (over y, core).
Axes of the slice: x: 4, y: 4, z: 16, core: 2. Of those that a mesh axis runs over, the one named last changes fastest.
Arguments:
- partials: bfloat16 [16384, 32768], P('dp', 'tensor'), may hold values from -6 to 6
- resid: bfloat16 [16384, 4096], P('dp', 'tensor'), may hold values from -6 to 6
- low: bfloat16 [16384, 4096], P('dp', 'tensor'), may hold values from -6 to 6
- mid: bfloat16 [16384, 4096], P('dp', 'tensor'), may hold values from -6 to 6
- joining: bfloat16 [3, 4096, 4096], P(None, 'tensor', 'dp'), may hold values from -0.0546875 to 0.0546875
- step_in: bfloat16 [4096, 128], replicated, may hold values from -0.09375 to 0.09375
- step_out: bfloat16 [128, 4096], replicated, may hold values from -0.5 to 0.5
- targets: bfloat16 [16384, 128], P('dp'), may hold values from -6 to 6
- lengths: int32 [64, 8], P('dp'), may hold values from 1 to 128, 256 in all within a row
- loss_mask: int32 [16384], P('dp'), may hold values 0 or 1
- dest: int32 [16384, 1], P('dp'), may hold values from 0 to 63; in each aligned block of 256 rows (0 to 255, 256 to 511, ...) at most 8 rows name the same one
Outputs:
- grad_start: float32 [32768, 4096], P(('dp', 'tensor'))
- final_state: bfloat16 [32768, 4096], P(('dp', 'tensor'))
The draws below stay inside these ranges and needn't reach their ends.
Inputs may be any that keep to these rules, and one draw needn't show every extreme that they name: `dest`: among the tokens of one sequence group no draft shard is named by more than 8 tokens, a bound that some block reaches. `lengths`: each row sums to 256; the longest is exactly 128.
All inputs are finite; a program needn't handle non-finite values. No bound on the sum of `loss_mask` on one device may be relied on, other than what follows from the above.
Results may differ from the reference program's by a relative error of at most 0.025.
Values may be sent and summed in bfloat16 or wider, within the bound.
No kernel may reach another device: no remote copies, remote signals or barrier semaphores. Data moves between devices by JAX's collectives and lax.ppermute only.
A program may use at most 128 MiB of HBM per device.

```python
import math
import jax
import jax.numpy as jnp
import numpy as np
from jax import lax

D = 4096
DW = 4096
HS = 128
TOK_DEV = 256
CONVS = 8
LMAX = 128
CAP = 8
TOKENS = 16384
SLOTS = 32768
N_DP = 64
N_TENSOR = 8


def with_ends(array, rng, low, top_value):
    dims = array.shape
    spot = [jax.random.randint(jax.random.fold_in(rng, axis), (), 0, dims[axis]) for axis in range(len(dims))]
    array = array.at[tuple(spot)].set(low)
    longest = dims.index(max(dims))
    spot[longest] = (spot[longest] + 1) % dims[longest]
    return array.at[tuple(spot)].set(top_value)


def steps_of(rng, dims, pieces, low, top_value):
    def one(position, shards_of):
        steps = jax.random.uniform(jax.random.fold_in(jax.random.fold_in(rng, 6), position), (shards_of,), jnp.float32, low / len(pieces), top_value / len(pieces))
        return jnp.repeat(jnp.exp(steps), dims[position] // shards_of).reshape((-1,) + (1,) * (len(dims) - position - 1))

    factor_of = one(*pieces[0])
    for cut in pieces[1:]:
        factor_of = factor_of * one(*cut)
    return factor_of


def profile(number_of, total, bound, slope):
    portions = [(1 << 20) // math.isqrt(rank ** slope) + 1 for rank in range(2, number_of + 1)]
    spare, holding = total - bound - (number_of - 1), [1] * (number_of - 1)
    while spare > 0:
        free = [i for i in range(number_of - 1) if holding[i] < bound]
        mass, budget = sum([portions[i] for i in free]), spare
        for i in free:
            extra = min(bound - holding[i], max(1, budget * portions[i] // mass), spare)
            holding[i] = holding[i] + extra
            spare = spare - extra
    return np.array([bound] + holding)


def uneven(key, count, total, bound, skew):
    if count == 2:
        one = jax.random.randint(key, (), max(1, total - bound), min(bound, total - 1) + 1)
        return jnp.stack([one, total - one])
    sizes = jnp.asarray(profile(count, total, bound, skew), jnp.int32)
    twos = (count - 1) // 2
    giver, sink = sizes[1:1 + 2 * twos:2], sizes[2:2 + 2 * twos:2]
    slack = jnp.minimum(giver - 1, bound - sink)
    shifted = jax.random.randint(jax.random.fold_in(key, 1), (twos,), 0, 1 << 20) % (slack + 1)
    sizes = sizes.at[1:1 + 2 * twos:2].set(giver - shifted).at[2:2 + 2 * twos:2].set(sink + shifted)
    return sizes[jax.random.permutation(jax.random.fold_in(key, 2), count)]


def deal_out(key, own, number, rows, number_of, top, most, lean):
    ranking = jax.random.permutation(key, number_of)
    packed, ordinary = load_shares(number_of, rows * top, most, lean, True), load_shares(number_of, rows * top, most, lean, False)
    places = jnp.arange(number_of)

    def named(sizes, offset_by):
        used = int((sizes > 0).sum())
        fixed = max(1, used // 4)
        shifted = fixed + (places - fixed + offset_by * (used - fixed)) % max(1, number_of - fixed)
        return jnp.zeros((number_of,), jnp.int32).at[ranking[jnp.where(places < fixed, places, shifted)]].set(jnp.asarray(sizes, jnp.int32))

    sizes = jnp.where(number % 4 == 0, named(packed, number // 4), named(ordinary, number - number // 4 - 1))
    mixed = jax.random.permutation(jax.random.fold_in(own, 3), number_of)
    giver, receiver = mixed[0:number_of // 2 * 2:2], mixed[1:number_of // 2 * 2:2]
    margin = jnp.minimum(sizes[giver] - 1, most - sizes[receiver]) // 2
    margin = jnp.where((giver == ranking[0]) | (receiver == ranking[0]) | (sizes[receiver] == 0), 0, jnp.maximum(margin, 0))
    shifted = jax.random.randint(jax.random.fold_in(own, 4), (number_of // 2,), 0, 1 << 20) % (margin + 1)
    sizes = sizes.at[giver].add(-shifted).at[receiver].add(shifted)
    members = jnp.searchsorted(jnp.cumsum(sizes), jnp.arange(rows * top), side="right").astype(jnp.int32)
    listing = members.reshape(top, rows).T
    listing = listing[jax.random.permutation(jax.random.fold_in(own, 1), rows)]
    offset_by = jax.random.randint(jax.random.fold_in(own, 2), (rows, 1), 0, top)
    return jnp.take_along_axis(listing, (jnp.arange(top)[None, :] + offset_by) % top, axis=1)


def load_shares(count, total, most, lean, full):
    portions = [(1 << 20) // math.isqrt(standing ** lean) + 1 for standing in range(1, count + 1)]
    largest = most if full else min(most, max(-(-total // count), total * portions[0] // sum(portions)))
    least = 1 if total - largest >= count - 1 else 0
    counts, spare = [largest] + [least] * (count - 1), total - largest - least * (count - 1)
    while spare > 0:
        movable = [i for i in range(1, count) if counts[i] < largest] or [i for i in range(1, count) if counts[i] < most]
        mass, left = sum([portions[i] for i in movable]), spare
        for i in movable:
            addition = min(most - counts[i], max(1, left * portions[i] // mass), spare)
            counts[i] = counts[i] + addition
            spare = spare - addition
    return np.array(counts)


def noise(own_key, dims, scale, most, shards=(), kind=jnp.bfloat16):
    level = steps_of(own_key, dims, shards, -0.22, 0.18) if shards else 1.0
    result = jax.random.normal(own_key, dims, jnp.float32) * scale * level
    return jnp.minimum(jnp.maximum(result, -most), most).astype(kind)


def setup_inputs(seed: int = 0) -> dict:
    streams_of = jax.random.split(jax.random.key(seed), 12)
    partials = noise(streams_of[0], (TOKENS, N_TENSOR * D), 0.5, 6.0, ((0, 64), (1, 8)))
    resid = noise(streams_of[1], (TOKENS, D), 1.0, 6.0, ((0, 64), (1, 8)))
    low = noise(streams_of[2], (TOKENS, D), 1.0, 6.0, ((0, 64), (1, 8)))
    mid = noise(streams_of[3], (TOKENS, D), 1.0, 6.0, ((0, 64), (1, 8)))
    joining = noise(streams_of[4], (3, D, DW), (3 * D) ** -0.5, 0.0546875, ((1, 8), (2, 64)))
    step_in = noise(streams_of[5], (DW, HS), DW ** -0.5, 0.09375)
    step_out = noise(streams_of[6], (HS, DW), HS ** -0.5, 0.5)
    targets = noise(streams_of[7], (TOKENS, HS), 1.0, 6.0, ((0, 64),))
    lengths = jax.vmap(lambda own: uneven(own, CONVS, TOK_DEV, LMAX, 2))(jax.random.split(streams_of[8], N_DP)).reshape((N_DP, CONVS)).astype(jnp.int32)
    loss_mask = with_ends((jax.random.randint(streams_of[9], (TOKENS,), 0, 4) < 3).astype(jnp.int32), jax.random.fold_in(streams_of[9], 1), 0, 1)
    dest_keys = jax.random.split(jax.random.fold_in(streams_of[10], 1), TOKENS // TOK_DEV)
    dest_turns = jax.random.permutation(jax.random.fold_in(streams_of[10], 3), TOKENS // TOK_DEV)
    dest = jax.vmap(lambda own, number: deal_out(jax.random.fold_in(streams_of[10], 2), own, number, TOK_DEV, N_DP, 1, CAP, 2))(dest_keys, dest_turns).reshape((TOKENS, 1))
    return {"partials": partials, "resid": resid, "low": low, "mid": mid, "joining": joining, "step_in": step_in, "step_out": step_out, "targets": targets, "lengths": lengths, "loss_mask": loss_mask, "dest": dest}


def remaining_steps(sizes, mask, count):
    ends = jnp.cumsum(sizes)
    starts = ends - sizes
    place = jnp.arange(count, dtype=jnp.int32)[:, None]
    inside = (place >= starts[None, :]) & (place < ends[None, :])
    offset = lax.optimization_barrier(jnp.sum(jnp.where(inside, place - starts[None, :], 0), axis=1))
    length = lax.optimization_barrier(jnp.sum(jnp.where(inside, sizes[None, :], 0), axis=1))
    return (jnp.minimum(length - 1 - offset, 3) * mask).astype(jnp.float32)

def draft_chain(step_in, step_out, start, goal, left):
    state = start
    saved = []
    for step in range(3):
        inv = lax.rsqrt(lax.optimization_barrier(jnp.mean(state * state, axis=-1, keepdims=True)) + 1e-06)
        normed = (state * inv).astype(jnp.bfloat16)
        pre = jnp.dot(normed, step_in, preferred_element_type=jnp.float32)
        active = jax.nn.silu(pre).astype(jnp.bfloat16)
        saved.append((state, inv, pre))
        state = state + jnp.dot(active, step_out, preferred_element_type=jnp.float32)
    target = goal.astype(jnp.float32)
    back = jnp.zeros(start.shape, jnp.float32)
    for step in (2, 1, 0):
        prev, inv, pre = saved[step]
        live = (left > step).astype(jnp.float32)
        dact = jnp.dot(back.astype(jnp.bfloat16), step_out.T, preferred_element_type=jnp.float32)
        sig = jax.nn.sigmoid(pre)
        dpre = (dact * (sig + pre * sig * (1.0 - sig)) + live * (pre - target)).astype(jnp.bfloat16)
        dnorm = jnp.dot(dpre, step_in.T, preferred_element_type=jnp.float32)
        back = back + inv * dnorm - prev * inv ** 3 * lax.optimization_barrier(jnp.mean(dnorm * prev, axis=-1, keepdims=True))
    return (state, back)

def reference(partials, resid, low, mid, joining, step_in, step_out, targets, lengths, loss_mask, dest):
    summed = resid.astype(jnp.float32)
    for block in range(N_TENSOR):
        summed = summed + partials[:, block * D:(block + 1) * D].astype(jnp.float32)
    high = summed.astype(jnp.bfloat16)
    width = D // N_TENSOR
    joined = jnp.zeros((TOKENS, DW), jnp.float32)
    for block in range(N_TENSOR):
        lo_col = block * width
        hi_col = (block + 1) * width
        term = jnp.dot(low[:, lo_col:hi_col], joining[0, lo_col:hi_col, :], preferred_element_type=jnp.float32)
        term = term + jnp.dot(mid[:, lo_col:hi_col], joining[1, lo_col:hi_col, :], preferred_element_type=jnp.float32)
        term = term + jnp.dot(high[:, lo_col:hi_col], joining[2, lo_col:hi_col, :], preferred_element_type=jnp.float32)
        term = lax.optimization_barrier(term.astype(jnp.bfloat16))
        joined = joined + term.astype(jnp.float32)
    joined = joined.astype(jnp.bfloat16)
    left = jax.vmap(lambda sizes, mask: remaining_steps(sizes, mask, TOK_DEV))(lengths, loss_mask.reshape(N_DP, TOK_DEV)).reshape(TOKENS)
    target = dest[:, 0].reshape(N_DP, TOK_DEV)
    hits = (target[:, :, None] == jnp.arange(N_DP, dtype=jnp.int32)[None, None, :]).astype(jnp.int32)
    rank = lax.optimization_barrier(jnp.sum(jnp.cumsum(hits, axis=1) * hits, axis=2)) - 1
    group = jnp.arange(N_DP, dtype=jnp.int32)[:, None]
    row = (target * (N_DP * CAP) + group * CAP + rank).reshape(TOKENS).astype(jnp.int32)
    start = jnp.zeros((SLOTS, DW), jnp.bfloat16).at[row].set(joined)
    goal = jnp.zeros((SLOTS, HS), jnp.bfloat16).at[row].set(targets)
    live = jnp.zeros((SLOTS, 1), jnp.float32).at[row].set(left[:, None])
    final, grad = draft_chain(step_in, step_out, start.astype(jnp.float32), goal, live)
    return (grad, final.astype(jnp.bfloat16))
```

```python
import jax
import jax.numpy as jnp
from jax import lax
from jax.experimental import pallas as pl
from jax.experimental.pallas import tpu as pltpu
from jax.sharding import Mesh, PartitionSpec as P

BF = jnp.bfloat16
F32 = jnp.float32
NT = (((1,), (1,)), ((), ()))
NN = (((1,), (0,)), ((), ()))
VMEM = pl.BlockSpec(memory_space=pltpu.VMEM)


def dot(a, b, dims=NN):
    return lax.dot_general(a, b, dims, preferred_element_type=F32)


def remaining_steps(sizes, mask, count):
    ends = jnp.cumsum(sizes)
    starts = ends - sizes
    place = jnp.arange(count, dtype=jnp.int32)[:, None]
    inside = (place >= starts[None, :]) & (place < ends[None, :])
    offset = jnp.sum(jnp.where(inside, place - starts[None, :], 0), axis=1)
    length = jnp.sum(jnp.where(inside, sizes[None, :], 0), axis=1)
    return (jnp.minimum(length - 1 - offset, 3) * mask).astype(F32)


def term_kernel(half_ref, pair_ref, high_ref, rows_ref, out_ref):
    weights = [rows_ref[0, :, 0, :, piece].reshape(256, 512) for piece in range(3)]
    for group in range(4):
        total = dot(pair_ref[group, 0:256], weights[0], NT)
        total += dot(pair_ref[group, 256:512], weights[1], NT)
        total += dot(high_ref[group], weights[2], NT)
        total = total.astype(BF)
        for part in range(2):
            out_ref[part, group * 256 : (group + 1) * 256, :] = total[:, part * 128 : (part + 1) * 128]


def term_half(half, pair, high, rows):
    return pl.pallas_call(
        term_kernel,
        grid_spec=pltpu.PrefetchScalarGridSpec(
            num_scalar_prefetch=1,
            grid=(2,),
            in_specs=[
                pl.BlockSpec((4, 528, 512), lambda i, h: (0, 0, 0)),
                pl.BlockSpec((4, 256, 512), lambda i, h: (0, 0, 0)),
                pl.BlockSpec((1, 2, 1, 2, 3, 64, 512), lambda i, h: (i, 0, h[0], 0, 0, 0, 0)),
            ],
            out_specs=pl.BlockSpec((2, 1024, 128), lambda i, h: (i, 0, 0)),
        ),
        out_shape=jax.ShapeDtypeStruct((4, 1024, 128), BF),
        compiler_params=pltpu.CompilerParams(vmem_limit_bytes=40 * 1024 * 1024),
        cost_estimate=pl.CostEstimate(
            flops=2 * 1024 * 1536 * 512, bytes_accessed=6 * 1024 * 1024, transcendentals=0
        ),
        name="term_half",
    )(half, pair, high, rows)


def spread_kernel(terms_ref, pair_ref, out_ref):
    total = terms_ref[0].astype(F32)
    for part in range(1, 4):
        total += terms_ref[part].astype(F32)
    joined = total.astype(BF)
    row = lax.broadcasted_iota(jnp.int32, (1024, 256), 0)
    for two in range(2):
        moved = None
        for group in (2 * two, 2 * two + 1):
            shard = pair_ref[group, 512:513, 0:256].astype(jnp.int32)
            rank = pair_ref[group, 512:513, 256:512].astype(jnp.int32)
            slot = shard * 16 + rank
            hot = jnp.where(row == slot, 1.0, 0.0).astype(BF)
            part = dot(hot, joined[group * 256 : (group + 1) * 256])
            moved = part if moved is None else moved + part
        out_ref[:, two * 16 : (two + 1) * 16, :] = moved.astype(BF).reshape(64, 16, 128)


def spread(terms, pair):
    return pl.pallas_call(
        spread_kernel,
        in_specs=[VMEM, VMEM],
        out_specs=VMEM,
        out_shape=jax.ShapeDtypeStruct((64, 32, 128), BF),
        compiler_params=pltpu.CompilerParams(vmem_limit_bytes=40 * 1024 * 1024),
        name="spread",
    )(terms, pair)


def chain_kernel(rows_ref, side_ref, in_ref, out_ref, grad_ref, final_ref, h0, h1, h2):
    for block in range(8):
        tiles = [
            jnp.concatenate([rows_ref[block, x], rows_ref[block, 4 + x]], axis=0).astype(F32)
            for x in range(4)
        ]
        for k in range(4):
            lane = (k // 2) * 64
            x = 2 * (k % 2)
            h0[:, block * 512 + k * 128 : block * 512 + (k + 1) * 128] = jnp.concatenate(
                [tiles[x][:, lane : lane + 64], tiles[x + 1][:, lane : lane + 64]], axis=1
            )
    side = side_ref[...].astype(F32)
    goal = side[:, 0:8, :].reshape(64, 128)
    left = side[:, 8:16, :].reshape(64, 128)
    states = (h0, h1, h2)
    invs, pres = [], []
    for step in range(3):
        state = states[step][...]
        inv = lax.rsqrt(jnp.sum(state * state, axis=-1, keepdims=True) * (1.0 / 4096) + 1e-06)
        pre = dot((state * inv).astype(BF), in_ref[...])
        active = (pre * jax.nn.sigmoid(pre)).astype(BF)
        invs.append(inv)
        pres.append(pre)
        after = state + dot(active, out_ref[...])
        if step < 2:
            states[step + 1][...] = after
        else:
            final_ref[...] = after.astype(BF)
    for step in (2, 1, 0):
        inv, pre = invs[step], pres[step]
        live = jnp.where(left > step, pre - goal, 0.0)
        if step == 2:
            dpre = live.astype(BF)
        else:
            dact = dot(grad_ref[...].astype(BF), out_ref[...], NT)
            sig = jax.nn.sigmoid(pre)
            dpre = (dact * (sig + pre * sig * (1.0 - sig)) + live).astype(BF)
        dnorm = dot(dpre, in_ref[...], NT)
        state = states[step][...]
        mean = jnp.sum(dnorm * state, axis=-1, keepdims=True) * (1.0 / 4096)
        back = inv * dnorm - state * (inv * inv * inv * mean)
        if step < 2:
            back = grad_ref[...] + back
        grad_ref[...] = back


def chain(rows, side, step_in, step_out):
    return pl.pallas_call(
        chain_kernel,
        in_specs=[VMEM] * 4,
        out_specs=[VMEM] * 2,
        out_shape=[
            jax.ShapeDtypeStruct((64, 4096), F32),
            jax.ShapeDtypeStruct((64, 4096), BF),
        ],
        scratch_shapes=[pltpu.VMEM((64, 4096), F32)] * 3,
        compiler_params=pltpu.CompilerParams(vmem_limit_bytes=40 * 1024 * 1024),
        name="chain",
    )(rows, side, step_in, step_out)


def per_device(
    partials, resid, low, mid, joining, step_in, step_out, targets, lengths, loss_mask, dest
):
    tensor = ("y", "c")
    dp = ("z", "x")
    rows = lax.all_gather(jnp.swapaxes(joining, 1, 2), "z")
    rows = rows.reshape(2, 2, 2, 2, 3, 64, 512)
    split = jnp.swapaxes(partials.reshape(256, 8, 512), 0, 1)
    summed = lax.psum_scatter(split, tensor, scatter_dimension=0, tiled=False).astype(F32)

    shard = dest[:, 0]
    earlier = jnp.arange(256)[:, None] > jnp.arange(256)[None, :]
    rank = jnp.sum(((shard[:, None] == shard[None, :]) & earlier).astype(jnp.int32), axis=1)
    place = lax.rem(lax.axis_index("x"), 2) * 8 + rank
    extra = jnp.concatenate([shard, place]).astype(BF)[None, :]
    extra = jnp.pad(extra, ((0, 15), (0, 0)))
    pair = jnp.concatenate([low, mid, extra], axis=0)
    pair = lax.all_to_all(
        jnp.broadcast_to(pair[None], (4, 528, 512)), "x", split_axis=0, concat_axis=0, tiled=True
    )

    left = remaining_steps(lengths[0], loss_mask, 256).astype(BF)
    side = jnp.concatenate([targets, jnp.broadcast_to(left[:, None], (256, 128))], axis=1)
    slot = jnp.arange(512, dtype=jnp.int32)[:, None] == (shard * 8 + rank)[None, :]
    side = jnp.dot(slot.astype(BF), side, preferred_element_type=F32).astype(BF)
    side = jnp.swapaxes(side.reshape(64, 8, 2, 128), 1, 2).reshape(64, 16, 128)
    side = lax.all_to_all(side, dp, split_axis=0, concat_axis=0, tiled=True)
    me = lax.axis_index("y") * 2 + lax.axis_index("c")
    side = lax.dynamic_slice_in_dim(side, me * 8, 8, 0)

    high = (summed + resid.astype(F32)).astype(BF)
    high = lax.all_to_all(
        jnp.broadcast_to(high[None], (4, 256, 512)), "x", split_axis=0, concat_axis=0, tiled=True
    )

    core = lax.axis_index("c").astype(jnp.int32).reshape(1)
    other = term_half(1 - core, pair, high, rows)
    other = lax.ppermute(other, "c", [(0, 1), (1, 0)])
    own = term_half(core, pair, high, rows)
    terms = (own.astype(F32) + other.astype(F32)).astype(BF)
    terms = lax.all_to_all(terms, "y", split_axis=0, concat_axis=0, tiled=True)
    moved = spread(terms, pair)
    moved = lax.all_to_all(moved, dp, split_axis=0, concat_axis=0, tiled=True)
    moved = lax.all_to_all(
        moved.reshape(8, 256, 128), tensor, split_axis=0, concat_axis=0, tiled=True
    )
    grad, final = chain(moved.reshape(8, 8, 32, 128), side, step_in, step_out)
    return (grad, final)


def solution(mesh):
    fine = Mesh(mesh.devices.reshape(16, 4, 4, 2), ("z", "x", "y", "c"))
    dp, tensor = ("z", "x"), ("y", "c")
    in_specs = (
        P(dp, tensor),
        P(dp, tensor),
        P(dp, tensor),
        P(dp, tensor),
        P(None, tensor, dp),
        P(),
        P(),
        P(dp, None),
        P(dp, None),
        P(dp),
        P(dp, None),
    )
    out_specs = (P(dp + tensor, None), P(dp + tensor, None))
    return jax.shard_map(
        per_device, mesh=fine, in_specs=in_specs, out_specs=out_specs, check_vma=False
    )
```

```python
import jax
import jax.numpy as jnp
from jax import lax
from jax.experimental import pallas as pl
from jax.experimental.pallas import tpu as pltpu
from jax.sharding import Mesh, PartitionSpec as P

BF = jnp.bfloat16
F32 = jnp.float32
NT = (((1,), (1,)), ((), ()))
NN = (((1,), (0,)), ((), ()))
VMEM = pl.BlockSpec(memory_space=pltpu.VMEM)


def dot(a, b, dims=NN):
    return lax.dot_general(a, b, dims, preferred_element_type=F32)


def remaining_steps(sizes, mask, count):
    ends = jnp.cumsum(sizes)
    starts = ends - sizes
    place = jnp.arange(count, dtype=jnp.int32)[:, None]
    inside = (place >= starts[None, :]) & (place < ends[None, :])
    offset = jnp.sum(jnp.where(inside, place - starts[None, :], 0), axis=1)
    length = jnp.sum(jnp.where(inside, sizes[None, :], 0), axis=1)
    return (jnp.minimum(length - 1 - offset, 3) * mask).astype(F32)


def split_kernel(in_ref, out_ref):
    out_ref[0] = in_ref[...]


def split_blocks(partials):
    return pl.pallas_call(
        split_kernel,
        grid=(8,),
        in_specs=[pl.BlockSpec((256, 512), lambda i: (0, i))],
        out_specs=pl.BlockSpec((1, 256, 512), lambda i: (i, 0, 0)),
        out_shape=jax.ShapeDtypeStruct((8, 256, 512), BF),
        name="split_blocks",
    )(partials)


def high_kernel(summed_ref, resid_ref, out_ref):
    high = (summed_ref[...].astype(F32) + resid_ref[...].astype(F32)).astype(BF)
    for x in range(4):
        out_ref[x] = high


def high_copies(summed, resid):
    return pl.pallas_call(
        high_kernel,
        in_specs=[VMEM, VMEM],
        out_specs=VMEM,
        out_shape=jax.ShapeDtypeStruct((4, 256, 512), BF),
        name="high_copies",
    )(summed, resid)


def term_kernel(half_ref, pair_ref, high_ref, rows_ref, out_ref, held, sems):
    half = half_ref[0]
    copies = [
        pltpu.make_async_copy(rows_ref.at[i, :, half], held.at[i], sems.at[i]) for i in range(2)
    ]
    for copy in copies:
        copy.start()
    for i in range(2):
        copies[i].wait()
        weights = [held[i, :, :, piece].reshape(256, 512) for piece in range(3)]
        for group in range(4):
            total = dot(pair_ref[group, 0:256], weights[0], NT)
            total += dot(pair_ref[group, 256:512], weights[1], NT)
            total += dot(high_ref[group], weights[2], NT)
            total = total.astype(BF)
            for part in range(2):
                out_ref[2 * i + part, group * 256 : (group + 1) * 256, :] = total[
                    :, part * 128 : (part + 1) * 128
                ]


def term_half(half, pair, high, rows):
    return pl.pallas_call(
        term_kernel,
        in_specs=[
            pl.BlockSpec(memory_space=pltpu.SMEM),
            VMEM,
            VMEM,
            pl.BlockSpec(memory_space=pltpu.HBM),
        ],
        out_specs=VMEM,
        out_shape=jax.ShapeDtypeStruct((4, 1024, 128), BF),
        scratch_shapes=[
            pltpu.VMEM((2, 2, 2, 3, 64, 512), BF),
            pltpu.SemaphoreType.DMA((2,)),
        ],
        compiler_params=pltpu.CompilerParams(vmem_limit_bytes=40 * 1024 * 1024),
        cost_estimate=pl.CostEstimate(
            flops=2 * 1024 * 1536 * 512, bytes_accessed=6 * 1024 * 1024, transcendentals=0
        ),
        name="term_half",
    )(half, pair, high, rows)


def spread_kernel(terms_ref, pair_ref, out_ref):
    total = terms_ref[0].astype(F32)
    for part in range(1, 4):
        total += terms_ref[part].astype(F32)
    joined = total.astype(BF)
    row = lax.broadcasted_iota(jnp.int32, (1024, 256), 0)
    for two in range(2):
        moved = None
        for group in (2 * two, 2 * two + 1):
            shard = pair_ref[group, 512:513, 0:256].astype(jnp.int32)
            rank = pair_ref[group, 512:513, 256:512].astype(jnp.int32)
            slot = shard * 16 + rank
            hot = jnp.where(row == slot, 1.0, 0.0).astype(BF)
            part = dot(hot, joined[group * 256 : (group + 1) * 256])
            moved = part if moved is None else moved + part
        out_ref[:, two * 16 : (two + 1) * 16, :] = moved.astype(BF).reshape(64, 16, 128)


def spread(terms, pair):
    return pl.pallas_call(
        spread_kernel,
        in_specs=[VMEM, VMEM],
        out_specs=VMEM,
        out_shape=jax.ShapeDtypeStruct((64, 32, 128), BF),
        compiler_params=pltpu.CompilerParams(vmem_limit_bytes=40 * 1024 * 1024),
        name="spread",
    )(terms, pair)


def chain_kernel(rows_ref, side_ref, in_ref, out_ref, grad_ref, final_ref, h0, h1, h2):
    for block in range(8):
        tiles = [
            jnp.concatenate([rows_ref[block, x], rows_ref[block, 4 + x]], axis=0).astype(F32)
            for x in range(4)
        ]
        for k in range(4):
            lane = (k // 2) * 64
            x = 2 * (k % 2)
            h0[:, block * 512 + k * 128 : block * 512 + (k + 1) * 128] = jnp.concatenate(
                [tiles[x][:, lane : lane + 64], tiles[x + 1][:, lane : lane + 64]], axis=1
            )
    side = side_ref[...].astype(F32)
    goal = side[:, 0:8, :].reshape(64, 128)
    left = side[:, 8:16, :].reshape(64, 128)
    states = (h0, h1, h2)
    invs, pres = [], []
    for step in range(3):
        state = states[step][...]
        inv = lax.rsqrt(jnp.sum(state * state, axis=-1, keepdims=True) * (1.0 / 4096) + 1e-06)
        pre = dot((state * inv).astype(BF), in_ref[...])
        active = (pre * jax.nn.sigmoid(pre)).astype(BF)
        invs.append(inv)
        pres.append(pre)
        after = state + dot(active, out_ref[...])
        if step < 2:
            states[step + 1][...] = after
        else:
            final_ref[...] = after.astype(BF)
    for step in (2, 1, 0):
        inv, pre = invs[step], pres[step]
        live = jnp.where(left > step, pre - goal, 0.0)
        if step == 2:
            dpre = live.astype(BF)
        else:
            dact = dot(grad_ref[...].astype(BF), out_ref[...], NT)
            sig = jax.nn.sigmoid(pre)
            dpre = (dact * (sig + pre * sig * (1.0 - sig)) + live).astype(BF)
        dnorm = dot(dpre, in_ref[...], NT)
        state = states[step][...]
        mean = jnp.sum(dnorm * state, axis=-1, keepdims=True) * (1.0 / 4096)
        back = inv * dnorm - state * (inv * inv * inv * mean)
        if step < 2:
            back = grad_ref[...] + back
        grad_ref[...] = back


def chain(rows, side, step_in, step_out):
    return pl.pallas_call(
        chain_kernel,
        in_specs=[VMEM] * 4,
        out_specs=[VMEM] * 2,
        out_shape=[
            jax.ShapeDtypeStruct((64, 4096), F32),
            jax.ShapeDtypeStruct((64, 4096), BF),
        ],
        scratch_shapes=[pltpu.VMEM((64, 4096), F32)] * 3,
        compiler_params=pltpu.CompilerParams(vmem_limit_bytes=40 * 1024 * 1024),
        name="chain",
    )(rows, side, step_in, step_out)


def per_device(
    partials, resid, low, mid, joining, step_in, step_out, targets, lengths, loss_mask, dest
):
    tensor = ("y", "c")
    dp = ("z", "x")
    rows = lax.all_gather(jnp.swapaxes(joining, 1, 2), "z")
    rows = rows.reshape(2, 2, 2, 2, 3, 64, 512)
    summed = lax.psum_scatter(
        split_blocks(partials), tensor, scatter_dimension=0, tiled=False
    )

    shard = dest[:, 0]
    earlier = jnp.arange(256)[:, None] > jnp.arange(256)[None, :]
    rank = jnp.sum(((shard[:, None] == shard[None, :]) & earlier).astype(jnp.int32), axis=1)
    place = lax.rem(lax.axis_index("x"), 2) * 8 + rank
    extra = jnp.concatenate([shard, place]).astype(BF)[None, :]
    extra = jnp.pad(extra, ((0, 15), (0, 0)))
    pair = jnp.concatenate([low, mid, extra], axis=0)
    pair = jnp.broadcast_to(pair[None], (4, 528, 512))

    left = remaining_steps(lengths[0], loss_mask, 256).astype(BF)
    side = jnp.concatenate([targets, jnp.broadcast_to(left[:, None], (256, 128))], axis=1)
    slot = jnp.arange(512, dtype=jnp.int32)[:, None] == (shard * 8 + rank)[None, :]
    side = jnp.dot(slot.astype(BF), side, preferred_element_type=F32).astype(BF)
    side = jnp.swapaxes(side.reshape(64, 8, 2, 128), 1, 2).reshape(64, 16, 128)
    side = lax.all_to_all(side, dp, split_axis=0, concat_axis=0, tiled=True)
    pair, side = lax.optimization_barrier((pair, side))
    pair = lax.all_to_all(pair, "x", split_axis=0, concat_axis=0, tiled=True)
    me = lax.axis_index("y") * 2 + lax.axis_index("c")
    side = lax.dynamic_slice_in_dim(side, me * 8, 8, 0)

    high = lax.all_to_all(
        high_copies(summed, resid), "x", split_axis=0, concat_axis=0, tiled=True
    )

    core = lax.axis_index("c").astype(jnp.int32).reshape(1)
    other = term_half(1 - core, pair, high, rows)
    other = lax.ppermute(other, "c", [(0, 1), (1, 0)])
    own = term_half(core, pair, high, rows)
    terms = (own.astype(F32) + other.astype(F32)).astype(BF)
    terms = lax.all_to_all(terms, "y", split_axis=0, concat_axis=0, tiled=True)
    moved = spread(terms, pair)
    moved = lax.all_to_all(moved, dp, split_axis=0, concat_axis=0, tiled=True)
    moved = lax.all_to_all(
        moved.reshape(8, 256, 128), tensor, split_axis=0, concat_axis=0, tiled=True
    )
    grad, final = chain(moved.reshape(8, 8, 32, 128), side, step_in, step_out)
    return (grad, final)


def solution(mesh):
    fine = Mesh(mesh.devices.reshape(16, 4, 4, 2), ("z", "x", "y", "c"))
    dp, tensor = ("z", "x"), ("y", "c")
    in_specs = (
        P(dp, tensor),
        P(dp, tensor),
        P(dp, tensor),
        P(dp, tensor),
        P(None, tensor, dp),
        P(),
        P(),
        P(dp, None),
        P(dp, None),
        P(dp),
        P(dp, None),
    )
    out_specs = (P(dp + tensor, None), P(dp + tensor, None))
    return jax.shard_map(
        per_device, mesh=fine, in_specs=in_specs, out_specs=out_specs, check_vma=False
    )
```

```python
import jax
import jax.numpy as jnp
from jax import lax
from jax.experimental import pallas as pl
from jax.experimental.pallas import tpu as pltpu
from jax.sharding import Mesh, PartitionSpec as P

BF = jnp.bfloat16
F32 = jnp.float32
NT = (((1,), (1,)), ((), ()))
NN = (((1,), (0,)), ((), ()))
VMEM = pl.BlockSpec(memory_space=pltpu.VMEM)
HBM = pl.BlockSpec(memory_space=pltpu.HBM)


def dot(a, b, dims=NN):
    return lax.dot_general(a, b, dims, preferred_element_type=F32)


def remaining_steps(sizes, mask, count):
    ends = jnp.cumsum(sizes)
    starts = ends - sizes
    place = jnp.arange(count, dtype=jnp.int32)[:, None]
    inside = (place >= starts[None, :]) & (place < ends[None, :])
    offset = jnp.sum(jnp.where(inside, place - starts[None, :], 0), axis=1)
    length = jnp.sum(jnp.where(inside, sizes[None, :], 0), axis=1)
    return (jnp.minimum(length - 1 - offset, 3) * mask).astype(F32)


def split_kernel(in_ref, out_ref, sems):
    copies = [
        pltpu.make_async_copy(in_ref.at[:, pl.ds(i * 512, 512)], out_ref.at[i], sems.at[i])
        for i in range(8)
    ]
    for copy in copies:
        copy.start()
    for copy in copies:
        copy.wait()


def split_blocks(partials):
    return pl.pallas_call(
        split_kernel,
        in_specs=[HBM],
        out_specs=HBM,
        out_shape=jax.ShapeDtypeStruct((8, 256, 512), BF),
        scratch_shapes=[pltpu.SemaphoreType.DMA((8,))],
        name="split_blocks",
    )(partials)


def high_kernel(summed_ref, resid_ref, out_ref):
    high = (summed_ref[...].astype(F32) + resid_ref[...].astype(F32)).astype(BF)
    for x in range(4):
        out_ref[x] = high


def high_copies(summed, resid):
    return pl.pallas_call(
        high_kernel,
        in_specs=[VMEM, VMEM],
        out_specs=VMEM,
        out_shape=jax.ShapeDtypeStruct((4, 256, 512), BF),
        name="high_copies",
    )(summed, resid)


def term_kernel(half_ref, p0, p1, p2, p3, high_ref, mine_ref, below_ref, above_ref, out_ref, held, sems):
    half = half_ref[0]
    copies = []
    for i, other in ((0, below_ref), (1, above_ref)):
        copies.append(
            (
                pltpu.make_async_copy(mine_ref.at[i, :, half], held.at[i, 0], sems.at[i, 0]),
                pltpu.make_async_copy(other.at[:, half], held.at[i, 1], sems.at[i, 1]),
            )
        )
    for two in copies:
        for copy in two:
            copy.start()
    for i in range(2):
        for copy in copies[i]:
            copy.wait()
        weights = [
            jnp.concatenate(
                [held[i, 0, 0, piece], held[i, 1, 0, piece], held[i, 0, 1, piece], held[i, 1, 1, piece]],
                axis=0,
            )
            for piece in range(3)
        ]
        for group, pair_ref in enumerate((p0, p1, p2, p3)):
            total = dot(pair_ref[0:256], weights[0], NT)
            total += dot(pair_ref[256:512], weights[1], NT)
            total += dot(high_ref[lax.rem(half_ref[1] + (4 - group), 4)], weights[2], NT)
            total = total.astype(BF)
            for part in range(2):
                out_ref[2 * i + part, group * 256 : (group + 1) * 256, :] = total[
                    :, part * 128 : (part + 1) * 128
                ]


def term_half(half, pairs, high, mine, below, above):
    return pl.pallas_call(
        term_kernel,
        in_specs=[pl.BlockSpec(memory_space=pltpu.SMEM)] + [VMEM] * 5 + [HBM] * 3,
        out_specs=VMEM,
        out_shape=jax.ShapeDtypeStruct((4, 1024, 128), BF),
        scratch_shapes=[
            pltpu.VMEM((2, 2, 2, 3, 64, 512), BF),
            pltpu.SemaphoreType.DMA((2, 2)),
        ],
        compiler_params=pltpu.CompilerParams(vmem_limit_bytes=40 * 1024 * 1024),
        cost_estimate=pl.CostEstimate(
            flops=2 * 1024 * 1536 * 512, bytes_accessed=6 * 1024 * 1024, transcendentals=0
        ),
        name="term_half",
    )(half, *pairs, high, mine, below, above)


def spread_kernel(terms_ref, p0, p1, p2, p3, out_ref):
    total = terms_ref[0].astype(F32)
    for part in range(1, 4):
        total += terms_ref[part].astype(F32)
    joined = total.astype(BF)
    row = lax.broadcasted_iota(jnp.int32, (1024, 256), 0)
    for two in range(2):
        moved = None
        for odd, pair_ref in enumerate(((p0, p1), (p2, p3))[two]):
            group = 2 * two + odd
            shard = pair_ref[512:513, 0:256].astype(jnp.int32)
            rank = pair_ref[512:513, 256:512].astype(jnp.int32)
            slot = shard * 16 + (odd * 8 + rank)
            hot = jnp.where(row == slot, 1.0, 0.0).astype(BF)
            part = dot(hot, joined[group * 256 : (group + 1) * 256])
            moved = part if moved is None else moved + part
        out_ref[:, two * 16 : (two + 1) * 16, :] = moved.astype(BF).reshape(64, 16, 128)


def spread(terms, pairs):
    return pl.pallas_call(
        spread_kernel,
        in_specs=[VMEM] * 5,
        out_specs=VMEM,
        out_shape=jax.ShapeDtypeStruct((64, 32, 128), BF),
        compiler_params=pltpu.CompilerParams(vmem_limit_bytes=40 * 1024 * 1024),
        name="spread",
    )(terms, *pairs)


def source_rows(tile, odd, x):
    tile = tile.astype(F32)
    tile = jnp.concatenate(
        [tile[8 * ((x - group) % 4) : 8 * ((x - group) % 4) + 8] for group in range(4)], axis=0
    )
    if odd:
        tile = jnp.concatenate([tile[:, 64:], tile[:, :64]], axis=1)
    return tile


def chain_kernel(rows_ref, goal_ref, left_ref, in_ref, out_ref, grad_ref, final_ref, h0, h1, h2):
    for block in range(8):
        tiles = [
            jnp.concatenate(
                [source_rows(rows_ref[block, 4 * odd + x], odd, x) for odd in range(2)], axis=0
            )
            for x in range(4)
        ]
        for k in range(4):
            lane = (k // 2) * 64
            x = 2 * (k % 2)
            h0[:, block * 512 + k * 128 : block * 512 + (k + 1) * 128] = jnp.concatenate(
                [tiles[x][:, lane : lane + 64], tiles[x + 1][:, lane : lane + 64]], axis=1
            )
    goal = goal_ref[...].astype(F32)
    left = left_ref[...].astype(F32)
    states = (h0, h1, h2)
    invs, pres = [], []
    for step in range(3):
        state = states[step][...]
        inv = lax.rsqrt(jnp.sum(state * state, axis=-1, keepdims=True) * (1.0 / 4096) + 1e-06)
        pre = dot((state * inv).astype(BF), in_ref[...])
        active = (pre * jax.nn.sigmoid(pre)).astype(BF)
        invs.append(inv)
        pres.append(pre)
        after = state + dot(active, out_ref[...])
        if step < 2:
            states[step + 1][...] = after
        else:
            final_ref[...] = after.astype(BF)
    for step in (2, 1, 0):
        inv, pre = invs[step], pres[step]
        live = jnp.where(left > step, pre - goal, 0.0)
        if step == 2:
            dpre = live.astype(BF)
        else:
            dact = dot(grad_ref[...].astype(BF), out_ref[...], NT)
            sig = jax.nn.sigmoid(pre)
            dpre = (dact * (sig + pre * sig * (1.0 - sig)) + live).astype(BF)
        dnorm = dot(dpre, in_ref[...], NT)
        state = states[step][...]
        mean = jnp.sum(dnorm * state, axis=-1, keepdims=True) * (1.0 / 4096)
        back = inv * dnorm - state * (inv * inv * inv * mean)
        if step < 2:
            back = grad_ref[...] + back
        grad_ref[...] = back


def chain(rows, goal, left, step_in, step_out):
    return pl.pallas_call(
        chain_kernel,
        in_specs=[VMEM] * 5,
        out_specs=[VMEM] * 2,
        out_shape=[
            jax.ShapeDtypeStruct((64, 4096), F32),
            jax.ShapeDtypeStruct((64, 4096), BF),
        ],
        scratch_shapes=[pltpu.VMEM((64, 4096), F32)] * 3,
        compiler_params=pltpu.CompilerParams(vmem_limit_bytes=40 * 1024 * 1024),
        name="chain",
    )(rows, goal, left, step_in, step_out)


def per_device(
    partials, resid, low, mid, joining, step_in, step_out, targets, lengths, loss_mask, dest
):
    tensor, dp, z = ("y", "c"), ("zh", "zl", "x"), ("zh", "zl")
    me = lax.axis_index("y") * 2 + lax.axis_index("c")
    core, along = lax.axis_index("c"), lax.axis_index("x")

    mine = lax.all_gather(jnp.swapaxes(joining, 1, 2), "zh")
    summed = lax.psum_scatter(split_blocks(partials), tensor, scatter_dimension=0, tiled=False)

    shard = dest[:, 0]
    earlier = jnp.arange(256)[:, None] > jnp.arange(256)[None, :]
    rank = jnp.sum(((shard[:, None] == shard[None, :]) & earlier).astype(jnp.int32), axis=1)
    extra = jnp.concatenate([shard, rank]).astype(BF)[None, :]
    extra = jnp.pad(extra, ((0, 15), (0, 0)))
    pair = jnp.concatenate([low, mid, extra], axis=0)
    pairs = [pair] + [lax.ppermute(pair, "x", ring(4, shift)) for shift in range(1, 4)]

    mine, *pairs = lax.optimization_barrier((mine, *pairs))
    below = lax.ppermute(mine[:4], z, ring(16, 1)).reshape(2, 2, 3, 64, 512)
    above = lax.ppermute(mine[4:], z, ring(16, -1)).reshape(2, 2, 3, 64, 512)
    mine = mine.reshape(2, 2, 2, 3, 64, 512)

    left = remaining_steps(lengths[0], loss_mask, 256).astype(BF)
    side = lax.dynamic_slice_in_dim(targets, me * 16, 16, 1)
    side = jnp.concatenate([side, jnp.broadcast_to(left[:, None], (256, 16))], axis=1)
    slot = jnp.arange(512, dtype=jnp.int32)[:, None] == (shard * 8 + rank)[None, :]
    side = jnp.dot(slot.astype(BF), side, preferred_element_type=F32).astype(BF)
    side = lax.all_to_all(side.reshape(64, 2, 128), dp, split_axis=0, concat_axis=0, tiled=True)
    side = lax.all_to_all(
        side.reshape(8, 16, 128), tensor, split_axis=0, concat_axis=0, tiled=True
    ).reshape(8, 64, 32)
    goal = jnp.swapaxes(side[:, :, :16], 0, 1).reshape(64, 128)
    left = jnp.broadcast_to(side[0, :, 16:17], (64, 128))

    high = high_copies(summed, resid)
    high, goal, left = lax.optimization_barrier((high, goal, left))
    high = lax.all_to_all(high, "x", split_axis=0, concat_axis=0, tiled=True)

    other = term_half(jnp.stack([1 - core, along]).astype(jnp.int32), pairs, high, mine, below, above)
    other = lax.ppermute(other, "c", ring(2, 1))
    own = term_half(jnp.stack([core, along]).astype(jnp.int32), pairs, high, mine, below, above)
    terms = (own.astype(F32) + other.astype(F32)).astype(BF)
    terms = lax.all_to_all(terms, "y", split_axis=0, concat_axis=0, tiled=True)
    moved = spread(terms, pairs)
    moved = lax.all_to_all(moved, dp, split_axis=0, concat_axis=0, tiled=True)
    moved = lax.all_to_all(
        moved.reshape(8, 256, 128), tensor, split_axis=0, concat_axis=0, tiled=True
    )
    grad, final = chain(moved.reshape(8, 8, 32, 128), goal, left, step_in, step_out)
    return (grad, final)


def ring(size, shift):
    return [(i, (i + shift) % size) for i in range(size)]


def solution(mesh):
    fine = Mesh(mesh.devices.reshape(8, 2, 4, 4, 2), ("zh", "zl", "x", "y", "c"))
    dp, tensor = ("zh", "zl", "x"), ("y", "c")
    in_specs = (
        P(dp, tensor),
        P(dp, tensor),
        P(dp, tensor),
        P(dp, tensor),
        P(None, tensor, dp),
        P(),
        P(),
        P(dp, None),
        P(dp, None),
        P(dp),
        P(dp, None),
    )
    out_specs = (P(dp + tensor, None), P(dp + tensor, None))
    return jax.shard_map(
        per_device, mesh=fine, in_specs=in_specs, out_specs=out_specs, check_vma=False
    )
```

```python
import functools

import jax
import jax.numpy as jnp
from jax import lax
from jax.experimental import pallas as pl
from jax.experimental.pallas import tpu as pltpu
from jax.sharding import Mesh, PartitionSpec as P

BF = jnp.bfloat16
F32 = jnp.float32
NT = (((1,), (1,)), ((), ()))
NN = (((1,), (0,)), ((), ()))
VMEM = pl.BlockSpec(memory_space=pltpu.VMEM)


def dot(a, b, dims=NN):
    return lax.dot_general(a, b, dims, preferred_element_type=F32)


def remaining_steps(sizes, mask, count):
    ends = jnp.cumsum(sizes)
    starts = ends - sizes
    place = jnp.arange(count, dtype=jnp.int32)[:, None]
    inside = (place >= starts[None, :]) & (place < ends[None, :])
    offset = jnp.sum(jnp.where(inside, place - starts[None, :], 0), axis=1)
    length = jnp.sum(jnp.where(inside, sizes[None, :], 0), axis=1)
    return (jnp.minimum(length - 1 - offset, 3) * mask).astype(F32)


SMEM = pl.BlockSpec(memory_space=pltpu.SMEM)
PLENTY = pltpu.CompilerParams(vmem_limit_bytes=40 * 1024 * 1024)


def blocks_at(place_ref, core, step):
    block = 2 * lax.rem(place_ref[2] + step, 4) + core
    return pl.ds(pl.multiple_of(block * 512, 512), 512)


def give_kernel(place_ref, partials_ref, out_ref):
    for step in range(4):
        out_ref[step] = partials_ref[:, blocks_at(place_ref, 1 - place_ref[0], step)]


def give_blocks(place, partials):
    return pl.pallas_call(
        give_kernel,
        in_specs=[SMEM, VMEM],
        out_specs=VMEM,
        out_shape=jax.ShapeDtypeStruct((4, 256, 512), BF),
        compiler_params=PLENTY,
        name="give_blocks",
    )(place, partials)


def pair_kernel(place_ref, partials_ref, other_ref, *out_refs):
    for step in range(4):
        own = partials_ref[:, blocks_at(place_ref, place_ref[0], step)].astype(F32)
        out_refs[step][...] = (own + other_ref[step].astype(F32)).astype(BF)


def pair_blocks(place, partials, other):
    return pl.pallas_call(
        pair_kernel,
        in_specs=[SMEM, VMEM, VMEM],
        out_specs=[VMEM] * 4,
        out_shape=[jax.ShapeDtypeStruct((256, 512), BF)] * 4,
        compiler_params=PLENTY,
        name="pair_blocks",
    )(place, partials, other)


def high_kernel(s0, s1, s2, s3, resid_ref, out_ref):
    total = s0[...].astype(F32) + s1[...].astype(F32) + s2[...].astype(F32) + s3[...].astype(F32)
    high = (total + resid_ref[...].astype(F32)).astype(BF)
    for x in range(4):
        out_ref[x] = high


def high_copies(sums, resid):
    return pl.pallas_call(
        high_kernel,
        in_specs=[VMEM] * 5,
        out_specs=VMEM,
        out_shape=jax.ShapeDtypeStruct((4, 256, 512), BF),
        name="high_copies",
    )(*sums, resid)


def term_kernel(other, place_ref, p0, p1, p2, p3, high_ref, rows_ref, out_ref):
    half = 1 - place_ref[0] if other else place_ref[0]
    weights = [
        jnp.concatenate(
            [rows_ref[lax.rem(place_ref[2] + step, 4), half, piece] for step in range(4)], axis=0
        )
        for piece in range(3)
    ]
    pairs = (p0, p1, p2, p3)

    def terms(group):
        pair_ref = pairs[group]
        total = dot(pair_ref[0:256], weights[0], NT)
        total += dot(pair_ref[256:512], weights[1], NT)
        return total + dot(high_ref[lax.rem(place_ref[1] + (4 - group), 4)], weights[2], NT)

    for low in range(2):
        left, right = terms(low), terms(low + 2)
        for step in range(4):
            cut = slice(step * 64, step * 64 + 64)
            out_ref[step, low * 256 : (low + 1) * 256, :] = jnp.concatenate(
                [left[:, cut], right[:, cut]], axis=1
            ).astype(BF)


def term_half(other, place, pairs, high, rows):
    return pl.pallas_call(
        functools.partial(term_kernel, other),
        in_specs=[SMEM] + [VMEM] * 6,
        out_specs=VMEM,
        out_shape=jax.ShapeDtypeStruct((4, 512, 128), BF),
        compiler_params=PLENTY,
        cost_estimate=pl.CostEstimate(
            flops=2 * 1024 * 1536 * 256, bytes_accessed=5 * 1024 * 1024, transcendentals=0
        ),
        name="term_half",
    )(place, *pairs, high, rows)


def spread_kernel(t0, t1, t2, t3, p0, p1, p2, p3, out_ref):
    total = t0[...].astype(F32) + t1[...].astype(F32) + t2[...].astype(F32) + t3[...].astype(F32)
    joined = total.astype(BF)
    row = lax.broadcasted_iota(jnp.int32, (1024, 256), 0)
    parts = []
    for group, pair_ref in enumerate((p0, p1, p2, p3)):
        low = group % 2
        shard = pair_ref[512:513, 0:256].astype(jnp.int32)
        rank = pair_ref[512:513, 256:512].astype(jnp.int32)
        hot = jnp.where(row == shard * 16 + (low * 8 + rank), 1.0, 0.0).astype(BF)
        parts.append(dot(hot, joined[low * 256 : (low + 1) * 256]))
    lane = lax.broadcasted_iota(jnp.int32, (1024, 128), 1)
    moved = jnp.where(lane < 64, parts[0] + parts[1], parts[2] + parts[3])
    out_ref[...] = moved.astype(BF).reshape(64, 16, 128)


def spread(terms, pairs):
    return pl.pallas_call(
        spread_kernel,
        in_specs=[VMEM] * 8,
        out_specs=VMEM,
        out_shape=jax.ShapeDtypeStruct((64, 16, 128), BF),
        compiler_params=PLENTY,
        name="spread",
    )(*terms, *pairs)


def source_rows(rows_ref, block, parity, x):
    pieces = []
    for odd in range(2):
        tile = rows_ref[block, 4 * odd + x].astype(F32)
        for group in range(4):
            came = (x - group) % 4
            low, right = came % 2, came // 2
            at = (parity ^ odd) * 16 + low * 8
            pieces.append(tile[at : at + 8, right * 64 : right * 64 + 64])
    return jnp.concatenate(pieces, axis=0)


def chain_kernel(rows_ref, in_ref, out_ref, grad_ref, final_ref, h0, h1, h2):
    for block in range(8):
        for k in range(4):
            x = 2 * (k % 2)
            h0[:, block * 512 + k * 128 : block * 512 + (k + 1) * 128] = jnp.concatenate(
                [
                    source_rows(rows_ref, block, k // 2, x),
                    source_rows(rows_ref, block, k // 2, x + 1),
                ],
                axis=1,
            )
    goals, lefts = [], []
    for source in range(8):
        sides = [rows_ref[block, source].astype(F32)[32:40] for block in range(8)]
        goals.append(jnp.concatenate([one[:, 0:16] for one in sides], axis=1))
        lefts.append(sides[0][:, 16:17])
    goal = jnp.concatenate(goals, axis=0)
    left = jnp.concatenate(lefts, axis=0)
    states = (h0, h1, h2)
    invs, pres = [], []
    for step in range(3):
        state = states[step][...]
        inv = lax.rsqrt(jnp.sum(state * state, axis=-1, keepdims=True) * (1.0 / 4096) + 1e-06)
        pre = dot((state * inv).astype(BF), in_ref[...])
        active = (pre * jax.nn.sigmoid(pre)).astype(BF)
        invs.append(inv)
        pres.append(pre)
        after = state + dot(active, out_ref[...])
        if step < 2:
            states[step + 1][...] = after
        else:
            final_ref[...] = after.astype(BF)
    for step in (2, 1, 0):
        inv, pre = invs[step], pres[step]
        live = jnp.where(left > step, pre - goal, 0.0)
        if step == 2:
            dpre = live.astype(BF)
        else:
            dact = dot(grad_ref[...].astype(BF), out_ref[...], NT)
            sig = jax.nn.sigmoid(pre)
            dpre = (dact * (sig + pre * sig * (1.0 - sig)) + live).astype(BF)
        dnorm = dot(dpre, in_ref[...], NT)
        state = states[step][...]
        mean = jnp.sum(dnorm * state, axis=-1, keepdims=True) * (1.0 / 4096)
        back = inv * dnorm - state * (inv * inv * inv * mean)
        if step < 2:
            back = grad_ref[...] + back
        grad_ref[...] = back


def chain(rows, step_in, step_out):
    return pl.pallas_call(
        chain_kernel,
        in_specs=[VMEM] * 3,
        out_specs=[VMEM] * 2,
        out_shape=[
            jax.ShapeDtypeStruct((64, 4096), F32),
            jax.ShapeDtypeStruct((64, 4096), BF),
        ],
        scratch_shapes=[pltpu.VMEM((64, 4096), F32)] * 3,
        compiler_params=pltpu.CompilerParams(vmem_limit_bytes=40 * 1024 * 1024),
        name="chain",
    )(rows, step_in, step_out)


def per_device(
    partials, resid, low, mid, joining, step_in, step_out, targets, lengths, loss_mask, dest
):
    tensor, dp = ("y", "c"), ("zh", "zl", "x")
    me = lax.axis_index("y") * 2 + lax.axis_index("c")
    place = jnp.stack([lax.axis_index("c"), lax.axis_index("x"), lax.axis_index("y")])
    place = place.astype(jnp.int32)

    mine = lax.all_gather(jnp.swapaxes(joining, 1, 2), "zh")

    other = lax.ppermute(give_blocks(place, partials), "c", ring(2, 1))
    sums = along_y(pair_blocks(place, partials, other))

    shard = dest[:, 0]
    earlier = jnp.arange(256)[:, None] > jnp.arange(256)[None, :]
    rank = jnp.sum(((shard[:, None] == shard[None, :]) & earlier).astype(jnp.int32), axis=1)
    extra = jnp.concatenate([shard, rank]).astype(BF)[None, :]
    extra = jnp.pad(extra, ((0, 15), (0, 0)))
    pair = jnp.concatenate([low, mid, extra], axis=0)
    pairs = [pair] + [lax.ppermute(pair, "x", ring(4, shift)) for shift in range(1, 4)]

    left = remaining_steps(lengths[0], loss_mask, 256).astype(BF)
    side = lax.dynamic_slice_in_dim(targets, me * 16, 16, 1)
    side = jnp.concatenate([side, jnp.broadcast_to(left[:, None], (256, 112))], axis=1)
    slot = jnp.arange(512, dtype=jnp.int32)[:, None] == (shard * 8 + rank)[None, :]
    side = jnp.dot(slot.astype(BF), side, preferred_element_type=F32).astype(BF)
    side = side.reshape(64, 8, 128)

    high = high_copies(sums, resid)
    high, side, *pairs = lax.optimization_barrier((high, side, *pairs))
    high = lax.all_to_all(high, "x", split_axis=0, concat_axis=0, tiled=True)

    swaps = [(2 * z + c, 2 * ((z + 1 - 2 * c) % 16) + c) for z in range(16) for c in range(2)]
    theirs = lax.ppermute(mine, ("zh", "zl", "c"), swaps)
    moved = []
    for rows in (mine, theirs):
        rows = rows.reshape(4, 2, 3, 64, 512)
        other = lax.ppermute(term_half(True, place, pairs, high, rows), "c", ring(2, 1))
        own = term_half(False, place, pairs, high, rows)
        terms = (own.astype(F32) + other.astype(F32)).astype(BF)
        terms = spread(along_y([terms[step] for step in range(4)]), pairs)
        if not moved:
            terms = jnp.concatenate([terms, side], axis=1)
        moved.append(lax.all_to_all(terms, dp, split_axis=0, concat_axis=0, tiled=True))
    moved = jnp.concatenate([moved[0][:, :16], moved[1], moved[0][:, 16:]], axis=1)
    moved = lax.all_to_all(
        moved.reshape(8, 8, 40, 128), tensor, split_axis=0, concat_axis=0, tiled=True
    )
    grad, final = chain(moved, step_in, step_out)
    return (grad, final)


def along_y(parts):
    return [parts[0]] + [lax.ppermute(parts[step], "y", ring(4, step)) for step in range(1, 4)]


def ring(size, shift):
    return [(i, (i + shift) % size) for i in range(size)]


def solution(mesh):
    fine = Mesh(mesh.devices.reshape(8, 2, 4, 4, 2), ("zh", "zl", "x", "y", "c"))
    dp, tensor = ("zh", "zl", "x"), ("y", "c")
    in_specs = (
        P(dp, tensor),
        P(dp, tensor),
        P(dp, tensor),
        P(dp, tensor),
        P(None, tensor, dp),
        P(),
        P(),
        P(dp, None),
        P(dp, None),
        P(dp),
        P(dp, None),
    )
    out_specs = (P(dp + tensor, None), P(dp + tensor, None))
    return jax.shard_map(
        per_device, mesh=fine, in_specs=in_specs, out_specs=out_specs, check_vma=False
    )
```

```python
import functools

import jax
import jax.numpy as jnp
from jax import lax
from jax.experimental import pallas as pl
from jax.experimental.pallas import tpu as pltpu
from jax.sharding import Mesh, PartitionSpec as P

BF = jnp.bfloat16
F32 = jnp.float32
NT = (((1,), (1,)), ((), ()))
NN = (((1,), (0,)), ((), ()))
VMEM = pl.BlockSpec(memory_space=pltpu.VMEM)


def dot(a, b, dims=NN):
    return lax.dot_general(a, b, dims, preferred_element_type=F32)


def remaining_steps(sizes, mask, count):
    ends = jnp.cumsum(sizes)
    starts = ends - sizes
    place = jnp.arange(count, dtype=jnp.int32)[:, None]
    inside = (place >= starts[None, :]) & (place < ends[None, :])
    offset = jnp.sum(jnp.where(inside, place - starts[None, :], 0), axis=1)
    length = jnp.sum(jnp.where(inside, sizes[None, :], 0), axis=1)
    return (jnp.minimum(length - 1 - offset, 3) * mask).astype(F32)


SMEM = pl.BlockSpec(memory_space=pltpu.SMEM)
PLENTY = pltpu.CompilerParams(vmem_limit_bytes=40 * 1024 * 1024)


def blocks_at(place_ref, core, step):
    block = 2 * lax.rem(place_ref[2] + step, 4) + core
    return pl.ds(pl.multiple_of(block * 512, 512), 512)


def give_kernel(place_ref, partials_ref, out_ref):
    for step in range(4):
        out_ref[step] = partials_ref[:, blocks_at(place_ref, 1 - place_ref[0], step)]


def give_blocks(place, partials):
    return pl.pallas_call(
        give_kernel,
        in_specs=[SMEM, VMEM],
        out_specs=VMEM,
        out_shape=jax.ShapeDtypeStruct((4, 256, 512), BF),
        compiler_params=PLENTY,
        name="give_blocks",
    )(place, partials)


def pair_kernel(place_ref, partials_ref, other_ref, *out_refs):
    for step in range(4):
        own = partials_ref[:, blocks_at(place_ref, place_ref[0], step)].astype(F32)
        out_refs[step][...] = (own + other_ref[step].astype(F32)).astype(BF)


def pair_blocks(place, partials, other):
    return pl.pallas_call(
        pair_kernel,
        in_specs=[SMEM, VMEM, VMEM],
        out_specs=[VMEM] * 4,
        out_shape=[jax.ShapeDtypeStruct((256, 512), BF)] * 4,
        compiler_params=PLENTY,
        name="pair_blocks",
    )(place, partials, other)


def high_kernel(s0, s1, s2, s3, resid_ref, out_ref):
    total = s0[...].astype(F32) + s1[...].astype(F32) + s2[...].astype(F32) + s3[...].astype(F32)
    high = (total + resid_ref[...].astype(F32)).astype(BF)
    for x in range(4):
        out_ref[x] = high


def high_copies(sums, resid):
    return pl.pallas_call(
        high_kernel,
        in_specs=[VMEM] * 5,
        out_specs=VMEM,
        out_shape=jax.ShapeDtypeStruct((4, 256, 512), BF),
        name="high_copies",
    )(*sums, resid)


def term_kernel(other, place_ref, p0, p1, p2, p3, high_ref, r0, r1, r2, r3, out_ref, held, sems):
    core, along, z = place_ref[0], place_ref[1], place_ref[3]
    half = 1 - core if other else core

    def away(block, odd):
        behind = z - (4 * block + 2 * half + odd)
        return lax.rem(jnp.where(core == 0, behind, -behind) + 32, 16)

    for odd in range(2):
        part = lax.rem(away(0, odd), 4)
        for k, rows_ref in enumerate((r0, r1, r2, r3)):

            @pl.when(part == k)
            def _(rows_ref=rows_ref):
                pltpu.make_async_copy(rows_ref, held.at[odd], sems.at[odd]).start()

    for odd in range(2):
        pltpu.make_async_copy(r0, held.at[odd], sems.at[odd]).wait()
    for two in range(2):
        weights = []
        for piece in range(3):
            weights.append(
                jnp.concatenate(
                    [
                        held[odd, lax.div(away(2 * two + block, odd), 4), piece]
                        for block in range(2)
                        for odd in range(2)
                    ],
                    axis=0,
                )
            )
        for group, pair_ref in enumerate((p0, p1, p2, p3)):
            total = dot(pair_ref[0:256], weights[0], NT)
            total += dot(pair_ref[256:512], weights[1], NT)
            total += dot(high_ref[lax.rem(along + (4 - group), 4)], weights[2], NT)
            total = total.astype(BF)
            for block in range(2):
                out_ref[2 * two + block, group * 256 : (group + 1) * 256, :] = total[
                    :, block * 128 : (block + 1) * 128
                ]


def term_half(other, place, pairs, high, rows):
    return pl.pallas_call(
        functools.partial(term_kernel, other),
        in_specs=[SMEM] + [VMEM] * 5 + [pl.BlockSpec(memory_space=pl.ANY)] * 4,
        out_specs=VMEM,
        out_shape=jax.ShapeDtypeStruct((4, 1024, 128), BF),
        scratch_shapes=[
            pltpu.VMEM((2, 4, 3, 64, 512), BF),
            pltpu.SemaphoreType.DMA((2,)),
        ],
        compiler_params=PLENTY,
        cost_estimate=pl.CostEstimate(
            flops=2 * 1024 * 1536 * 512, bytes_accessed=6 * 1024 * 1024, transcendentals=0
        ),
        name="term_half",
    )(place, *pairs, high, *rows)


def spread_kernel(terms_ref, p0, p1, p2, p3, out_ref):
    total = terms_ref[0].astype(F32)
    for part in range(1, 4):
        total += terms_ref[part].astype(F32)
    joined = total.astype(BF)
    row = lax.broadcasted_iota(jnp.int32, (1024, 256), 0)
    for two in range(2):
        moved = None
        for odd, pair_ref in enumerate(((p0, p1), (p2, p3))[two]):
            group = 2 * two + odd
            shard = pair_ref[512:513, 0:256].astype(jnp.int32)
            rank = pair_ref[512:513, 256:512].astype(jnp.int32)
            slot = shard * 16 + (odd * 8 + rank)
            hot = jnp.where(row == slot, 1.0, 0.0).astype(BF)
            part = dot(hot, joined[group * 256 : (group + 1) * 256])
            moved = part if moved is None else moved + part
        out_ref[:, two * 16 : (two + 1) * 16, :] = moved.astype(BF).reshape(64, 16, 128)


def spread(terms, pairs):
    return pl.pallas_call(
        spread_kernel,
        in_specs=[VMEM] * 5,
        out_specs=VMEM,
        out_shape=jax.ShapeDtypeStruct((64, 32, 128), BF),
        compiler_params=PLENTY,
        name="spread",
    )(terms, *pairs)


def source_rows(tile, x):
    tile = tile.astype(F32)
    order = [8 * ((x - group) % 4) for group in range(4)]
    return [tile[at : at + 8] for at in order]


def chain_kernel(rows_ref, in_ref, out_ref, grad_ref, final_ref, h0, h1, h2):
    for block in range(8):
        tiles = [
            jnp.concatenate(
                source_rows(rows_ref[block, x], x) + source_rows(rows_ref[block, 4 + x], x), axis=0
            )
            for x in range(4)
        ]
        for k in range(4):
            lane = (k // 2) * 64
            x = 2 * (k % 2)
            h0[:, block * 512 + k * 128 : block * 512 + (k + 1) * 128] = jnp.concatenate(
                [tiles[x][:, lane : lane + 64], tiles[x + 1][:, lane : lane + 64]], axis=1
            )
    goals, lefts = [], []
    for source in range(8):
        sides = [rows_ref[block, source].astype(F32)[32:40] for block in range(8)]
        goals.append(jnp.concatenate([one[:, 0:16] for one in sides], axis=1))
        lefts.append(sides[0][:, 16:17])
    goal = jnp.concatenate(goals, axis=0)
    left = jnp.concatenate(lefts, axis=0)
    states = (h0, h1, h2)
    invs, pres = [], []
    for step in range(3):
        state = states[step][...]
        inv = lax.rsqrt(jnp.sum(state * state, axis=-1, keepdims=True) * (1.0 / 4096) + 1e-06)
        pre = dot((state * inv).astype(BF), in_ref[...])
        active = (pre * jax.nn.sigmoid(pre)).astype(BF)
        invs.append(inv)
        pres.append(pre)
        after = state + dot(active, out_ref[...])
        if step < 2:
            states[step + 1][...] = after
        else:
            final_ref[...] = after.astype(BF)
    for step in (2, 1, 0):
        inv, pre = invs[step], pres[step]
        live = jnp.where(left > step, pre - goal, 0.0)
        if step == 2:
            dpre = live.astype(BF)
        else:
            dact = dot(grad_ref[...].astype(BF), out_ref[...], NT)
            sig = jax.nn.sigmoid(pre)
            dpre = (dact * (sig + pre * sig * (1.0 - sig)) + live).astype(BF)
        dnorm = dot(dpre, in_ref[...], NT)
        state = states[step][...]
        mean = jnp.sum(dnorm * state, axis=-1, keepdims=True) * (1.0 / 4096)
        back = inv * dnorm - state * (inv * inv * inv * mean)
        if step < 2:
            back = grad_ref[...] + back
        grad_ref[...] = back


def chain(rows, step_in, step_out):
    return pl.pallas_call(
        chain_kernel,
        in_specs=[VMEM] * 3,
        out_specs=[VMEM] * 2,
        out_shape=[
            jax.ShapeDtypeStruct((64, 4096), F32),
            jax.ShapeDtypeStruct((64, 4096), BF),
        ],
        scratch_shapes=[pltpu.VMEM((64, 4096), F32)] * 3,
        compiler_params=PLENTY,
        name="chain",
    )(rows, step_in, step_out)


def per_device(
    partials, resid, low, mid, joining, step_in, step_out, targets, lengths, loss_mask, dest
):
    tensor, dp = ("y", "c"), ("z", "x")
    me = lax.axis_index("y") * 2 + lax.axis_index("c")
    place = jnp.stack([lax.axis_index(axis) for axis in ("c", "x", "y", "z")]).astype(jnp.int32)

    quarter = [jnp.swapaxes(joining, 1, 2)]
    for _ in range(3):
        quarter.append(along_z(quarter[-1], 4))
    rows = [jnp.stack(quarter)]
    for _ in range(3):
        rows.append(along_z(rows[-1], 1))

    other = lax.ppermute(give_blocks(place, partials), "c", ring(2, 1))
    sums = along_y(pair_blocks(place, partials, other))

    shard = dest[:, 0]
    earlier = jnp.arange(256)[:, None] > jnp.arange(256)[None, :]
    rank = jnp.sum(((shard[:, None] == shard[None, :]) & earlier).astype(jnp.int32), axis=1)
    extra = jnp.concatenate([shard, rank]).astype(BF)[None, :]
    extra = jnp.pad(extra, ((0, 15), (0, 0)))
    pair = jnp.concatenate([low, mid, extra], axis=0)
    pairs = [pair] + [lax.ppermute(pair, "x", ring(4, shift)) for shift in range(1, 4)]

    left = remaining_steps(lengths[0], loss_mask, 256).astype(BF)
    side = lax.dynamic_slice_in_dim(targets, me * 16, 16, 1)
    side = jnp.concatenate([side, jnp.broadcast_to(left[:, None], (256, 112))], axis=1)
    slot = jnp.arange(512, dtype=jnp.int32)[:, None] == (shard * 8 + rank)[None, :]
    side = jnp.dot(slot.astype(BF), side, preferred_element_type=F32).astype(BF)
    side = side.reshape(64, 8, 128)

    high = high_copies(sums, resid)
    high, side, *pairs = lax.optimization_barrier((high, side, *pairs))
    high = lax.all_to_all(high, "x", split_axis=0, concat_axis=0, tiled=True)

    other = lax.ppermute(term_half(True, place, pairs, high, rows), "c", ring(2, 1))
    own = term_half(False, place, pairs, high, rows)
    terms = (own.astype(F32) + other.astype(F32)).astype(BF)
    terms = lax.all_to_all(terms, "y", split_axis=0, concat_axis=0, tiled=True)
    moved = jnp.concatenate([spread(terms, pairs), side], axis=1)
    moved = lax.all_to_all(moved, dp, split_axis=0, concat_axis=0, tiled=True)
    moved = lax.all_to_all(
        moved.reshape(8, 8, 40, 128), tensor, split_axis=0, concat_axis=0, tiled=True
    )
    grad, final = chain(moved, step_in, step_out)
    return (grad, final)


def along_y(parts):
    return [parts[0]] + [lax.ppermute(parts[step], "y", ring(4, step)) for step in range(1, 4)]


def along_z(part, step):
    pairs = [(2 * z + c, 2 * ((z + step * (1 - 2 * c)) % 16) + c) for z in range(16) for c in range(2)]
    return lax.ppermute(part, ("z", "c"), pairs)


def ring(size, shift):
    return [(i, (i + shift) % size) for i in range(size)]


def solution(mesh):
    fine = Mesh(mesh.devices.reshape(16, 4, 4, 2), ("z", "x", "y", "c"))
    dp, tensor = ("z", "x"), ("y", "c")
    in_specs = (
        P(dp, tensor),
        P(dp, tensor),
        P(dp, tensor),
        P(dp, tensor),
        P(None, tensor, dp),
        P(),
        P(),
        P(dp, None),
        P(dp, None),
        P(dp),
        P(dp, None),
    )
    out_specs = (P(dp + tensor, None), P(dp + tensor, None))
    return jax.shard_map(
        per_device, mesh=fine, in_specs=in_specs, out_specs=out_specs, check_vma=False
    )
```

```python
import jax
import jax.numpy as jnp
from jax import lax
from jax.experimental import pallas as pl
from jax.experimental.pallas import tpu as pltpu
from jax.sharding import Mesh, PartitionSpec as P

BF = jnp.bfloat16
F32 = jnp.float32
NT = (((1,), (1,)), ((), ()))
NN = (((1,), (0,)), ((), ()))
VMEM = pl.BlockSpec(memory_space=pltpu.VMEM)
HBM = pl.BlockSpec(memory_space=pltpu.HBM)


def dot(a, b, dims=NN):
    return lax.dot_general(a, b, dims, preferred_element_type=F32)


def remaining_steps(sizes, mask, count):
    ends = jnp.cumsum(sizes)
    starts = ends - sizes
    place = jnp.arange(count, dtype=jnp.int32)[:, None]
    inside = (place >= starts[None, :]) & (place < ends[None, :])
    offset = jnp.sum(jnp.where(inside, place - starts[None, :], 0), axis=1)
    length = jnp.sum(jnp.where(inside, sizes[None, :], 0), axis=1)
    return (jnp.minimum(length - 1 - offset, 3) * mask).astype(F32)


def high_kernel(summed_ref, resid_ref, out_ref):
    for block in range(8):
        total = summed_ref[:, block * 512 : (block + 1) * 512].astype(F32)
        high = (total + resid_ref[block].astype(F32)).astype(BF)
        for x in range(4):
            out_ref[8 * x + block] = high


def high_copies(summed, resid):
    return pl.pallas_call(
        high_kernel,
        in_specs=[VMEM, VMEM],
        out_specs=VMEM,
        out_shape=jax.ShapeDtypeStruct((32, 32, 512), BF),
        name="high_copies",
    )(summed, resid)


def term_kernel(half_ref, p0, p1, p2, p3, high_ref, rows_ref, out_ref, held, sems):
    half = half_ref[0]
    copies = [
        pltpu.make_async_copy(rows_ref.at[i, :, half], held.at[i], sems.at[i]) for i in range(2)
    ]
    for copy in copies:
        copy.start()
    for i in range(2):
        copies[i].wait()
        weights = [held[i, :, :, piece].reshape(256, 512) for piece in range(3)]
        for group, pair_ref in enumerate((p0, p1, p2, p3)):
            total = dot(pair_ref[0:256], weights[0], NT)
            total += dot(pair_ref[256:512], weights[1], NT)
            total += dot(high_ref[lax.rem(half_ref[1] + (4 - group), 4)], weights[2], NT)
            total = total.astype(BF)
            for part in range(2):
                out_ref[2 * i + part, group * 256 : (group + 1) * 256, :] = total[
                    :, part * 128 : (part + 1) * 128
                ]


def term_half(half, pairs, high, rows):
    return pl.pallas_call(
        term_kernel,
        in_specs=[pl.BlockSpec(memory_space=pltpu.SMEM)] + [VMEM] * 5 + [HBM],
        out_specs=VMEM,
        out_shape=jax.ShapeDtypeStruct((4, 1024, 128), BF),
        scratch_shapes=[
            pltpu.VMEM((2, 2, 2, 3, 64, 512), BF),
            pltpu.SemaphoreType.DMA((2,)),
        ],
        compiler_params=pltpu.CompilerParams(vmem_limit_bytes=40 * 1024 * 1024),
        cost_estimate=pl.CostEstimate(
            flops=2 * 1024 * 1536 * 512, bytes_accessed=6 * 1024 * 1024, transcendentals=0
        ),
        name="term_half",
    )(half, *pairs, high, rows)


def spread_kernel(terms_ref, p0, p1, p2, p3, out_ref):
    total = terms_ref[0].astype(F32)
    for part in range(1, 4):
        total += terms_ref[part].astype(F32)
    joined = total.astype(BF)
    row = lax.broadcasted_iota(jnp.int32, (1024, 256), 0)
    for two in range(2):
        moved = None
        for odd, pair_ref in enumerate(((p0, p1), (p2, p3))[two]):
            group = 2 * two + odd
            shard = pair_ref[512:513, 0:256].astype(jnp.int32)
            rank = pair_ref[512:513, 256:512].astype(jnp.int32)
            slot = shard * 16 + (odd * 8 + rank)
            hot = jnp.where(row == slot, 1.0, 0.0).astype(BF)
            part = dot(hot, joined[group * 256 : (group + 1) * 256])
            moved = part if moved is None else moved + part
        out_ref[:, two * 16 : (two + 1) * 16, :] = moved.astype(BF).reshape(64, 16, 128)


def spread(terms, pairs):
    return pl.pallas_call(
        spread_kernel,
        in_specs=[VMEM] * 5,
        out_specs=VMEM,
        out_shape=jax.ShapeDtypeStruct((64, 32, 128), BF),
        compiler_params=pltpu.CompilerParams(vmem_limit_bytes=40 * 1024 * 1024),
        name="spread",
    )(terms, *pairs)


def source_rows(tile, x):
    tile = tile.astype(F32)
    order = [8 * ((x - group) % 4) for group in range(4)]
    return [tile[at : at + 8] for at in order]


def chain_kernel(rows_ref, goal_ref, left_ref, in_ref, out_ref, grad_ref, final_ref, h0, h1, h2):
    for block in range(8):
        tiles = [
            jnp.concatenate(
                source_rows(rows_ref[block, x], x) + source_rows(rows_ref[block, 4 + x], x), axis=0
            )
            for x in range(4)
        ]
        for k in range(4):
            lane = (k // 2) * 64
            x = 2 * (k % 2)
            h0[:, block * 512 + k * 128 : block * 512 + (k + 1) * 128] = jnp.concatenate(
                [tiles[x][:, lane : lane + 64], tiles[x + 1][:, lane : lane + 64]], axis=1
            )
    goal = goal_ref[...].astype(F32)
    left = left_ref[...].astype(F32)
    states = (h0, h1, h2)
    invs, pres = [], []
    for step in range(3):
        state = states[step][...]
        inv = lax.rsqrt(jnp.sum(state * state, axis=-1, keepdims=True) * (1.0 / 4096) + 1e-06)
        pre = dot((state * inv).astype(BF), in_ref[...])
        active = (pre * jax.nn.sigmoid(pre)).astype(BF)
        invs.append(inv)
        pres.append(pre)
        after = state + dot(active, out_ref[...])
        if step < 2:
            states[step + 1][...] = after
        else:
            final_ref[...] = after.astype(BF)
    for step in (2, 1, 0):
        inv, pre = invs[step], pres[step]
        live = jnp.where(left > step, pre - goal, 0.0)
        if step == 2:
            dpre = live.astype(BF)
        else:
            dact = dot(grad_ref[...].astype(BF), out_ref[...], NT)
            sig = jax.nn.sigmoid(pre)
            dpre = (dact * (sig + pre * sig * (1.0 - sig)) + live).astype(BF)
        dnorm = dot(dpre, in_ref[...], NT)
        state = states[step][...]
        mean = jnp.sum(dnorm * state, axis=-1, keepdims=True) * (1.0 / 4096)
        back = inv * dnorm - state * (inv * inv * inv * mean)
        if step < 2:
            back = grad_ref[...] + back
        grad_ref[...] = back


def chain(rows, goal, left, step_in, step_out):
    return pl.pallas_call(
        chain_kernel,
        in_specs=[VMEM] * 5,
        out_specs=[VMEM] * 2,
        out_shape=[
            jax.ShapeDtypeStruct((64, 4096), F32),
            jax.ShapeDtypeStruct((64, 4096), BF),
        ],
        scratch_shapes=[pltpu.VMEM((64, 4096), F32)] * 3,
        compiler_params=pltpu.CompilerParams(vmem_limit_bytes=40 * 1024 * 1024),
        name="chain",
    )(rows, goal, left, step_in, step_out)


def per_device(
    partials, resid, low, mid, joining, step_in, step_out, targets, lengths, loss_mask, dest
):
    tensor, dp, z = ("y", "c"), ("z", "x"), "z"
    me = lax.axis_index("y") * 2 + lax.axis_index("c")
    core, along = lax.axis_index("c"), lax.axis_index("x")

    rows = lax.all_gather(jnp.swapaxes(joining, 1, 2), z).reshape(2, 2, 2, 2, 3, 64, 512)
    summed = lax.psum_scatter(partials, tensor, scatter_dimension=0, tiled=True)
    resid = lax.all_to_all(
        resid.reshape(8, 32, 512), tensor, split_axis=0, concat_axis=0, tiled=True
    )

    shard = dest[:, 0]
    earlier = jnp.arange(256)[:, None] > jnp.arange(256)[None, :]
    rank = jnp.sum(((shard[:, None] == shard[None, :]) & earlier).astype(jnp.int32), axis=1)
    extra = jnp.concatenate([shard, rank]).astype(BF)[None, :]
    extra = jnp.pad(extra, ((0, 15), (0, 0)))
    pair = jnp.concatenate([low, mid, extra], axis=0)
    pairs = [pair] + [lax.ppermute(pair, "x", ring(4, shift)) for shift in range(1, 4)]

    left = remaining_steps(lengths[0], loss_mask, 256).astype(BF)
    side = lax.dynamic_slice_in_dim(targets, me * 16, 16, 1)
    side = jnp.concatenate([side, jnp.broadcast_to(left[:, None], (256, 16))], axis=1)
    slot = jnp.arange(512, dtype=jnp.int32)[:, None] == (shard * 8 + rank)[None, :]
    side = jnp.dot(slot.astype(BF), side, preferred_element_type=F32).astype(BF)
    side = lax.all_to_all(side.reshape(64, 2, 128), dp, split_axis=0, concat_axis=0, tiled=True)
    side = lax.all_to_all(
        side.reshape(8, 16, 128), tensor, split_axis=0, concat_axis=0, tiled=True
    ).reshape(8, 64, 32)
    goal = jnp.swapaxes(side[:, :, :16], 0, 1).reshape(64, 128)
    left = jnp.broadcast_to(side[0, :, 16:17], (64, 128))

    high = high_copies(summed, resid)
    high, goal, left, *pairs = lax.optimization_barrier((high, goal, left, *pairs))
    high = lax.all_to_all(high, ("x",) + tensor, split_axis=0, concat_axis=0, tiled=True)
    high = high.reshape(4, 256, 512)

    other = term_half(jnp.stack([1 - core, along]).astype(jnp.int32), pairs, high, rows)
    other = lax.ppermute(other, "c", ring(2, 1))
    own = term_half(jnp.stack([core, along]).astype(jnp.int32), pairs, high, rows)
    terms = (own.astype(F32) + other.astype(F32)).astype(BF)
    terms = lax.all_to_all(terms, "y", split_axis=0, concat_axis=0, tiled=True)
    moved = spread(terms, pairs)
    moved = lax.all_to_all(moved, dp, split_axis=0, concat_axis=0, tiled=True)
    moved = lax.all_to_all(
        moved.reshape(8, 256, 128), tensor, split_axis=0, concat_axis=0, tiled=True
    )
    grad, final = chain(moved.reshape(8, 8, 32, 128), goal, left, step_in, step_out)
    return (grad, final)


def ring(size, shift):
    return [(i, (i + shift) % size) for i in range(size)]


def solution(mesh):
    fine = Mesh(mesh.devices.reshape(16, 4, 4, 2), ("z", "x", "y", "c"))
    dp, tensor = ("z", "x"), ("y", "c")
    in_specs = (
        P(dp, tensor),
        P(dp, tensor),
        P(dp, tensor),
        P(dp, tensor),
        P(None, tensor, dp),
        P(),
        P(),
        P(dp, None),
        P(dp, None),
        P(dp),
        P(dp, None),
    )
    out_specs = (P(dp + tensor, None), P(dp + tensor, None))
    return jax.shard_map(
        per_device, mesh=fine, in_specs=in_specs, out_specs=out_specs, check_vma=False
    )
```

```python
import jax
import jax.numpy as jnp
from jax import lax
from jax.experimental import pallas as pl
from jax.experimental.pallas import tpu as pltpu
from jax.sharding import Mesh, PartitionSpec as P

BF = jnp.bfloat16
F32 = jnp.float32
NT = (((1,), (1,)), ((), ()))
NN = (((1,), (0,)), ((), ()))
VMEM = pl.BlockSpec(memory_space=pltpu.VMEM)
HBM = pl.BlockSpec(memory_space=pltpu.HBM)


def dot(a, b, dims=NN):
    return lax.dot_general(a, b, dims, preferred_element_type=F32)


def remaining_steps(sizes, mask, count):
    ends = jnp.cumsum(sizes)
    starts = ends - sizes
    place = jnp.arange(count, dtype=jnp.int32)[:, None]
    inside = (place >= starts[None, :]) & (place < ends[None, :])
    offset = jnp.sum(jnp.where(inside, place - starts[None, :], 0), axis=1)
    length = jnp.sum(jnp.where(inside, sizes[None, :], 0), axis=1)
    return (jnp.minimum(length - 1 - offset, 3) * mask).astype(F32)


def high_kernel(summed_ref, resid_ref, out_ref):
    for block in range(8):
        total = summed_ref[:, block * 512 : (block + 1) * 512].astype(F32)
        high = (total + resid_ref[block].astype(F32)).astype(BF)
        for x in range(4):
            out_ref[8 * x + block] = high


def high_copies(summed, resid):
    return pl.pallas_call(
        high_kernel,
        in_specs=[VMEM, VMEM],
        out_specs=VMEM,
        out_shape=jax.ShapeDtypeStruct((32, 32, 512), BF),
        name="high_copies",
    )(summed, resid)


def term_kernel(half_ref, p0, p1, p2, p3, high_ref, rows_ref, out_ref, held, sems):
    half = half_ref[0]
    copies = [
        pltpu.make_async_copy(rows_ref.at[i, :, half], held.at[i], sems.at[i]) for i in range(2)
    ]
    for copy in copies:
        copy.start()
    for i in range(2):
        copies[i].wait()
        weights = [held[i, :, :, piece].reshape(256, 512) for piece in range(3)]
        for group, pair_ref in enumerate((p0, p1, p2, p3)):
            total = dot(pair_ref[0:256], weights[0], NT)
            total += dot(pair_ref[256:512], weights[1], NT)
            total += dot(high_ref[lax.rem(half_ref[1] + (4 - group), 4)], weights[2], NT)
            total = total.astype(BF)
            for part in range(2):
                out_ref[2 * i + part, group * 256 : (group + 1) * 256, :] = total[
                    :, part * 128 : (part + 1) * 128
                ]


def term_half(half, pairs, high, rows):
    return pl.pallas_call(
        term_kernel,
        in_specs=[pl.BlockSpec(memory_space=pltpu.SMEM)] + [VMEM] * 5 + [HBM],
        out_specs=VMEM,
        out_shape=jax.ShapeDtypeStruct((4, 1024, 128), BF),
        scratch_shapes=[
            pltpu.VMEM((2, 2, 2, 3, 64, 512), BF),
            pltpu.SemaphoreType.DMA((2,)),
        ],
        compiler_params=pltpu.CompilerParams(vmem_limit_bytes=40 * 1024 * 1024),
        cost_estimate=pl.CostEstimate(
            flops=2 * 1024 * 1536 * 512, bytes_accessed=6 * 1024 * 1024, transcendentals=0
        ),
        name="term_half",
    )(half, *pairs, high, rows)


def spread_kernel(terms_ref, p0, p1, p2, p3, out_ref):
    total = terms_ref[0].astype(F32)
    for part in range(1, 4):
        total += terms_ref[part].astype(F32)
    joined = total.astype(BF)
    row = lax.broadcasted_iota(jnp.int32, (1024, 256), 0)
    for two in range(2):
        moved = None
        for odd, pair_ref in enumerate(((p0, p1), (p2, p3))[two]):
            group = 2 * two + odd
            shard = pair_ref[512:513, 0:256].astype(jnp.int32)
            rank = pair_ref[512:513, 256:512].astype(jnp.int32)
            slot = shard * 16 + (odd * 8 + rank)
            hot = jnp.where(row == slot, 1.0, 0.0).astype(BF)
            part = dot(hot, joined[group * 256 : (group + 1) * 256])
            moved = part if moved is None else moved + part
        out_ref[:, two * 16 : (two + 1) * 16, :] = moved.astype(BF).reshape(64, 16, 128)


def spread(terms, pairs):
    return pl.pallas_call(
        spread_kernel,
        in_specs=[VMEM] * 5,
        out_specs=VMEM,
        out_shape=jax.ShapeDtypeStruct((64, 32, 128), BF),
        compiler_params=pltpu.CompilerParams(vmem_limit_bytes=40 * 1024 * 1024),
        name="spread",
    )(terms, *pairs)


def source_rows(tile, x):
    tile = tile.astype(F32)
    order = [8 * ((x - group) % 4) for group in range(4)]
    return [tile[at : at + 8] for at in order]


def chain_kernel(rows_ref, goal_ref, left_ref, in_ref, out_ref, grad_ref, final_ref, h0, h1, h2):
    for block in range(8):
        tiles = [
            jnp.concatenate(
                source_rows(rows_ref[block, x], x) + source_rows(rows_ref[block, 4 + x], x), axis=0
            )
            for x in range(4)
        ]
        for k in range(4):
            lane = (k // 2) * 64
            x = 2 * (k % 2)
            h0[:, block * 512 + k * 128 : block * 512 + (k + 1) * 128] = jnp.concatenate(
                [tiles[x][:, lane : lane + 64], tiles[x + 1][:, lane : lane + 64]], axis=1
            )
    goal = goal_ref[...].astype(F32)
    left = left_ref[...].astype(F32)
    states = (h0, h1, h2)
    invs, pres = [], []
    for step in range(3):
        state = states[step][...]
        inv = lax.rsqrt(jnp.sum(state * state, axis=-1, keepdims=True) * (1.0 / 4096) + 1e-06)
        pre = dot((state * inv).astype(BF), in_ref[...])
        active = (pre * jax.nn.sigmoid(pre)).astype(BF)
        invs.append(inv)
        pres.append(pre)
        after = state + dot(active, out_ref[...])
        if step < 2:
            states[step + 1][...] = after
        else:
            final_ref[...] = after.astype(BF)
    for step in (2, 1, 0):
        inv, pre = invs[step], pres[step]
        live = jnp.where(left > step, pre - goal, 0.0)
        if step == 2:
            dpre = live.astype(BF)
        else:
            dact = dot(grad_ref[...].astype(BF), out_ref[...], NT)
            sig = jax.nn.sigmoid(pre)
            dpre = (dact * (sig + pre * sig * (1.0 - sig)) + live).astype(BF)
        dnorm = dot(dpre, in_ref[...], NT)
        state = states[step][...]
        mean = jnp.sum(dnorm * state, axis=-1, keepdims=True) * (1.0 / 4096)
        back = inv * dnorm - state * (inv * inv * inv * mean)
        if step < 2:
            back = grad_ref[...] + back
        grad_ref[...] = back


def chain(rows, goal, left, step_in, step_out):
    return pl.pallas_call(
        chain_kernel,
        in_specs=[VMEM] * 5,
        out_specs=[VMEM] * 2,
        out_shape=[
            jax.ShapeDtypeStruct((64, 4096), F32),
            jax.ShapeDtypeStruct((64, 4096), BF),
        ],
        scratch_shapes=[pltpu.VMEM((64, 4096), F32)] * 3,
        compiler_params=pltpu.CompilerParams(vmem_limit_bytes=40 * 1024 * 1024),
        name="chain",
    )(rows, goal, left, step_in, step_out)


def per_device(
    partials, resid, low, mid, joining, step_in, step_out, targets, lengths, loss_mask, dest
):
    tensor, dp, z = ("y", "c"), ("z", "x"), "z"
    me = lax.axis_index("y") * 2 + lax.axis_index("c")
    core, along = lax.axis_index("c"), lax.axis_index("x")

    rows = lax.all_gather(jnp.swapaxes(joining, 1, 2), z).reshape(2, 2, 2, 2, 3, 64, 512)
    summed = lax.psum_scatter(partials, tensor, scatter_dimension=0, tiled=True)
    resid = lax.all_to_all(
        resid.reshape(8, 32, 512), tensor, split_axis=0, concat_axis=0, tiled=True
    )

    shard = dest[:, 0]
    earlier = jnp.arange(256)[:, None] > jnp.arange(256)[None, :]
    rank = jnp.sum(((shard[:, None] == shard[None, :]) & earlier).astype(jnp.int32), axis=1)
    extra = jnp.concatenate([shard, rank]).astype(BF)[None, :]
    extra = jnp.pad(extra, ((0, 15), (0, 0)))
    pair = jnp.concatenate([low, mid, extra], axis=0)
    pairs = [pair] + [lax.ppermute(pair, "x", ring(4, shift)) for shift in range(1, 4)]

    left = remaining_steps(lengths[0], loss_mask, 256).astype(BF)
    side = lax.dynamic_slice_in_dim(targets, me * 16, 16, 1)
    side = jnp.concatenate([side, jnp.broadcast_to(left[:, None], (256, 16))], axis=1)
    slot = jnp.arange(512, dtype=jnp.int32)[:, None] == (shard * 8 + rank)[None, :]
    side = jnp.dot(slot.astype(BF), side, preferred_element_type=F32).astype(BF)
    resid, side = lax.optimization_barrier((resid, side))
    side = lax.all_to_all(side.reshape(64, 2, 128), dp, split_axis=0, concat_axis=0, tiled=True)

    high = high_copies(summed, resid)
    high, side, *pairs = lax.optimization_barrier((high, side, *pairs))
    high = lax.all_to_all(high, ("x",) + tensor, split_axis=0, concat_axis=0, tiled=True)
    high, side = lax.optimization_barrier((high, side))
    side = lax.all_to_all(
        side.reshape(8, 16, 128), tensor, split_axis=0, concat_axis=0, tiled=True
    ).reshape(8, 64, 32)
    goal = jnp.swapaxes(side[:, :, :16], 0, 1).reshape(64, 128)
    left = jnp.broadcast_to(side[0, :, 16:17], (64, 128))
    high, goal, left = lax.optimization_barrier((high, goal, left))
    high = high.reshape(4, 256, 512)

    other = term_half(jnp.stack([1 - core, along]).astype(jnp.int32), pairs, high, rows)
    other = lax.ppermute(other, "c", ring(2, 1))
    own = term_half(jnp.stack([core, along]).astype(jnp.int32), pairs, high, rows)
    terms = (own.astype(F32) + other.astype(F32)).astype(BF)
    terms = lax.all_to_all(terms, "y", split_axis=0, concat_axis=0, tiled=True)
    moved = spread(terms, pairs)
    moved = lax.all_to_all(moved, dp, split_axis=0, concat_axis=0, tiled=True)
    moved = lax.all_to_all(
        moved.reshape(8, 256, 128), tensor, split_axis=0, concat_axis=0, tiled=True
    )
    grad, final = chain(moved.reshape(8, 8, 32, 128), goal, left, step_in, step_out)
    return (grad, final)


def ring(size, shift):
    return [(i, (i + shift) % size) for i in range(size)]


def solution(mesh):
    fine = Mesh(mesh.devices.reshape(16, 4, 4, 2), ("z", "x", "y", "c"))
    dp, tensor = ("z", "x"), ("y", "c")
    in_specs = (
        P(dp, tensor),
        P(dp, tensor),
        P(dp, tensor),
        P(dp, tensor),
        P(None, tensor, dp),
        P(),
        P(),
        P(dp, None),
        P(dp, None),
        P(dp),
        P(dp, None),
    )
    out_specs = (P(dp + tensor, None), P(dp + tensor, None))
    return jax.shard_map(
        per_device, mesh=fine, in_specs=in_specs, out_specs=out_specs, check_vma=False
    )
```

```python
import functools

import jax
import jax.numpy as jnp
from jax import lax
from jax.experimental import pallas as pl
from jax.experimental.pallas import tpu as pltpu
from jax.sharding import Mesh, PartitionSpec as P

BF = jnp.bfloat16
F32 = jnp.float32
NT = (((1,), (1,)), ((), ()))
NN = (((1,), (0,)), ((), ()))
VMEM = pl.BlockSpec(memory_space=pltpu.VMEM)
HBM = pl.BlockSpec(memory_space=pltpu.HBM)


def dot(a, b, dims=NN):
    return lax.dot_general(a, b, dims, preferred_element_type=F32)


def remaining_steps(sizes, mask, count):
    ends = jnp.cumsum(sizes)
    starts = ends - sizes
    place = jnp.arange(count, dtype=jnp.int32)[:, None]
    inside = (place >= starts[None, :]) & (place < ends[None, :])
    offset = jnp.sum(jnp.where(inside, place - starts[None, :], 0), axis=1)
    length = jnp.sum(jnp.where(inside, sizes[None, :], 0), axis=1)
    return (jnp.minimum(length - 1 - offset, 3) * mask).astype(F32)


def high_kernel(summed_ref, resid_ref, out_ref):
    for block in range(8):
        total = summed_ref[:, block * 512 : (block + 1) * 512].astype(F32)
        high = (total + resid_ref[block].astype(F32)).astype(BF)
        for x in range(4):
            out_ref[8 * x + block] = high


def high_copies(summed, resid):
    return pl.pallas_call(
        high_kernel,
        in_specs=[VMEM, VMEM],
        out_specs=VMEM,
        out_shape=jax.ShapeDtypeStruct((32, 32, 512), BF),
        name="high_copies",
    )(summed, resid)


FIRST, SECOND = (1, 3), (3, 1)


def term_kernel(other, give, place_ref, p0, p1, p2, p3, high_ref, rows_ref, out_ref, held, sems):
    half = 1 - place_ref[0] if other else place_ref[0]
    first = 1 + 2 * half
    y = place_ref[2]
    blocks = (y ^ first, y ^ 2) if give else (y, y ^ first ^ 2)
    copies = [
        pltpu.make_async_copy(rows_ref.at[block, half], held.at[i], sems.at[i])
        for i, block in enumerate(blocks)
    ]
    for copy in copies:
        copy.start()
    for copy in copies:
        copy.wait()
    weights = [held[:, :, piece].reshape(256, 512) for piece in range(3)]
    for group, pair_ref in enumerate((p0, p1, p2, p3)):
        total = dot(pair_ref[0:256], weights[0], NT)
        total += dot(pair_ref[256:512], weights[1], NT)
        total += dot(high_ref[lax.rem(place_ref[1] + (4 - group), 4)], weights[2], NT)
        total = total.astype(BF)
        for i in range(2):
            out_ref[i, group * 256 : (group + 1) * 256, :] = total[:, i * 128 : (i + 1) * 128]


def term_half(other, give, place, pairs, high, rows):
    return pl.pallas_call(
        functools.partial(term_kernel, other, give),
        in_specs=[pl.BlockSpec(memory_space=pltpu.SMEM)] + [VMEM] * 5 + [HBM],
        out_specs=VMEM,
        out_shape=jax.ShapeDtypeStruct((2, 1024, 128), BF),
        scratch_shapes=[
            pltpu.VMEM((2, 2, 3, 64, 512), BF),
            pltpu.SemaphoreType.DMA((2,)),
        ],
        compiler_params=pltpu.CompilerParams(vmem_limit_bytes=40 * 1024 * 1024),
        cost_estimate=pl.CostEstimate(
            flops=2 * 1024 * 1536 * 256, bytes_accessed=5 * 1024 * 1024, transcendentals=0
        ),
        name="term_half",
    )(place, *pairs, high, rows)


def spread_kernel(t0, t1, t2, t3, p0, p1, p2, p3, out_ref):
    total = t0[0].astype(F32) + t1[0].astype(F32) + t2[0].astype(F32) + t3[...].astype(F32)
    joined = total.astype(BF)
    row = lax.broadcasted_iota(jnp.int32, (1024, 256), 0)
    for two in range(2):
        moved = None
        for odd, pair_ref in enumerate(((p0, p1), (p2, p3))[two]):
            group = 2 * two + odd
            shard = pair_ref[512:513, 0:256].astype(jnp.int32)
            rank = pair_ref[512:513, 256:512].astype(jnp.int32)
            slot = shard * 16 + (odd * 8 + rank)
            hot = jnp.where(row == slot, 1.0, 0.0).astype(BF)
            part = dot(hot, joined[group * 256 : (group + 1) * 256])
            moved = part if moved is None else moved + part
        out_ref[:, two * 16 : (two + 1) * 16, :] = moved.astype(BF).reshape(64, 16, 128)


def spread(terms, pairs):
    return pl.pallas_call(
        spread_kernel,
        in_specs=[VMEM] * 8,
        out_specs=VMEM,
        out_shape=jax.ShapeDtypeStruct((64, 32, 128), BF),
        compiler_params=pltpu.CompilerParams(vmem_limit_bytes=40 * 1024 * 1024),
        name="spread",
    )(*terms, *pairs)


def source_rows(tile, x):
    tile = tile.astype(F32)
    order = [8 * ((x - group) % 4) for group in range(4)]
    return [tile[at : at + 8] for at in order]


def chain_kernel(rows_ref, goal_ref, left_ref, in_ref, out_ref, grad_ref, final_ref, h0, h1, h2):
    for block in range(8):
        tiles = [
            jnp.concatenate(
                source_rows(rows_ref[block, x], x) + source_rows(rows_ref[block, 4 + x], x), axis=0
            )
            for x in range(4)
        ]
        for k in range(4):
            lane = (k // 2) * 64
            x = 2 * (k % 2)
            h0[:, block * 512 + k * 128 : block * 512 + (k + 1) * 128] = jnp.concatenate(
                [tiles[x][:, lane : lane + 64], tiles[x + 1][:, lane : lane + 64]], axis=1
            )
    goal = goal_ref[...].astype(F32)
    left = left_ref[...].astype(F32)
    states = (h0, h1, h2)
    invs, pres = [], []
    for step in range(3):
        state = states[step][...]
        inv = lax.rsqrt(jnp.sum(state * state, axis=-1, keepdims=True) * (1.0 / 4096) + 1e-06)
        pre = dot((state * inv).astype(BF), in_ref[...])
        active = (pre * jax.nn.sigmoid(pre)).astype(BF)
        invs.append(inv)
        pres.append(pre)
        after = state + dot(active, out_ref[...])
        if step < 2:
            states[step + 1][...] = after
        else:
            final_ref[...] = after.astype(BF)
    for step in (2, 1, 0):
        inv, pre = invs[step], pres[step]
        live = jnp.where(left > step, pre - goal, 0.0)
        if step == 2:
            dpre = live.astype(BF)
        else:
            dact = dot(grad_ref[...].astype(BF), out_ref[...], NT)
            sig = jax.nn.sigmoid(pre)
            dpre = (dact * (sig + pre * sig * (1.0 - sig)) + live).astype(BF)
        dnorm = dot(dpre, in_ref[...], NT)
        state = states[step][...]
        mean = jnp.sum(dnorm * state, axis=-1, keepdims=True) * (1.0 / 4096)
        back = inv * dnorm - state * (inv * inv * inv * mean)
        if step < 2:
            back = grad_ref[...] + back
        grad_ref[...] = back


def chain(rows, goal, left, step_in, step_out):
    return pl.pallas_call(
        chain_kernel,
        in_specs=[VMEM] * 5,
        out_specs=[VMEM] * 2,
        out_shape=[
            jax.ShapeDtypeStruct((64, 4096), F32),
            jax.ShapeDtypeStruct((64, 4096), BF),
        ],
        scratch_shapes=[pltpu.VMEM((64, 4096), F32)] * 3,
        compiler_params=pltpu.CompilerParams(vmem_limit_bytes=40 * 1024 * 1024),
        name="chain",
    )(rows, goal, left, step_in, step_out)


def per_device(
    partials, resid, low, mid, joining, step_in, step_out, targets, lengths, loss_mask, dest
):
    tensor, dp, z = ("y", "c"), ("z", "x"), "z"
    me = lax.axis_index("y") * 2 + lax.axis_index("c")
    place = jnp.stack([lax.axis_index(axis) for axis in ("c", "x", "y")]).astype(jnp.int32)

    rows = lax.all_gather(jnp.swapaxes(joining, 1, 2), z).reshape(4, 2, 2, 3, 64, 512)
    summed = lax.psum_scatter(partials, tensor, scatter_dimension=0, tiled=True)
    resid = lax.all_to_all(
        resid.reshape(8, 32, 512), tensor, split_axis=0, concat_axis=0, tiled=True
    )

    shard = dest[:, 0]
    earlier = jnp.arange(256)[:, None] > jnp.arange(256)[None, :]
    rank = jnp.sum(((shard[:, None] == shard[None, :]) & earlier).astype(jnp.int32), axis=1)
    extra = jnp.concatenate([shard, rank]).astype(BF)[None, :]
    extra = jnp.pad(extra, ((0, 15), (0, 0)))
    pair = jnp.concatenate([low, mid, extra], axis=0)
    pairs = [pair] + [lax.ppermute(pair, "x", ring(4, shift)) for shift in range(1, 4)]

    left = remaining_steps(lengths[0], loss_mask, 256).astype(BF)
    side = lax.dynamic_slice_in_dim(targets, me * 16, 16, 1)
    side = jnp.concatenate([side, jnp.broadcast_to(left[:, None], (256, 16))], axis=1)
    slot = jnp.arange(512, dtype=jnp.int32)[:, None] == (shard * 8 + rank)[None, :]
    side = jnp.dot(slot.astype(BF), side, preferred_element_type=F32).astype(BF)
    resid, side = lax.optimization_barrier((resid, side))
    side = lax.all_to_all(side.reshape(64, 2, 128), dp, split_axis=0, concat_axis=0, tiled=True)

    high = high_copies(summed, resid)
    high, side, *pairs = lax.optimization_barrier((high, side, *pairs))
    high = lax.all_to_all(high, ("x",) + tensor, split_axis=0, concat_axis=0, tiled=True)
    high, side = lax.optimization_barrier((high, side))
    side = lax.all_to_all(
        side.reshape(8, 16, 128), tensor, split_axis=0, concat_axis=0, tiled=True
    )
    high, side = lax.optimization_barrier((high, side))
    side = side.reshape(8, 64, 32)
    goal = jnp.swapaxes(side[:, :, :16], 0, 1).reshape(64, 128)
    left = jnp.broadcast_to(side[0, :, 16:17], (64, 128))
    high = high.reshape(4, 256, 512)

    def both(give, place):
        other = term_half(True, give, place, pairs, high, rows)
        return term_half(False, give, place, pairs, high, rows), lax.ppermute(other, "c", ring(2, 1))

    own, other = both(True, place)
    given = (own.astype(F32) + other.astype(F32)).astype(BF)
    given, place = lax.optimization_barrier((given, place))
    given = meet(given, FIRST)
    own, other = both(False, place)
    second = own[1].astype(F32) + other[1].astype(F32) + given[1].astype(F32)
    second = meet(second.astype(BF), SECOND)
    moved = spread((own, other, given, second), pairs)
    moved = lax.all_to_all(moved, dp, split_axis=0, concat_axis=0, tiled=True)
    moved = lax.all_to_all(
        moved.reshape(8, 256, 128), tensor, split_axis=0, concat_axis=0, tiled=True
    )
    grad, final = chain(moved.reshape(8, 8, 32, 128), goal, left, step_in, step_out)
    return (grad, final)


def meet(part, steps):
    pairs = [(2 * y + c, 2 * (y ^ steps[c]) + c) for y in range(4) for c in range(2)]
    return lax.ppermute(part, ("y", "c"), pairs)


def ring(size, shift):
    return [(i, (i + shift) % size) for i in range(size)]


def solution(mesh):
    fine = Mesh(mesh.devices.reshape(16, 4, 4, 2), ("z", "x", "y", "c"))
    dp, tensor = ("z", "x"), ("y", "c")
    in_specs = (
        P(dp, tensor),
        P(dp, tensor),
        P(dp, tensor),
        P(dp, tensor),
        P(None, tensor, dp),
        P(),
        P(),
        P(dp, None),
        P(dp, None),
        P(dp),
        P(dp, None),
    )
    out_specs = (P(dp + tensor, None), P(dp + tensor, None))
    return jax.shard_map(
        per_device, mesh=fine, in_specs=in_specs, out_specs=out_specs, check_vma=False
    )
```

```python
import jax
import jax.numpy as jnp
from jax import lax
from jax.experimental import pallas as pl
from jax.experimental.pallas import tpu as pltpu
from jax.sharding import Mesh, PartitionSpec as P

BF = jnp.bfloat16
F32 = jnp.float32
NT = (((1,), (1,)), ((), ()))
NN = (((1,), (0,)), ((), ()))
VMEM = pl.BlockSpec(memory_space=pltpu.VMEM)


def dot(a, b, dims=NN):
    return lax.dot_general(a, b, dims, preferred_element_type=F32)


def remaining_steps(sizes, mask, count):
    ends = jnp.cumsum(sizes)
    starts = ends - sizes
    place = jnp.arange(count, dtype=jnp.int32)[:, None]
    inside = (place >= starts[None, :]) & (place < ends[None, :])
    offset = jnp.sum(jnp.where(inside, place - starts[None, :], 0), axis=1)
    length = jnp.sum(jnp.where(inside, sizes[None, :], 0), axis=1)
    return (jnp.minimum(length - 1 - offset, 3) * mask).astype(F32)


def high_kernel(summed_ref, resid_ref, out_ref):
    for block in range(8):
        total = summed_ref[:, block * 512 : (block + 1) * 512].astype(F32)
        high = (total + resid_ref[block].astype(F32)).astype(BF)
        for x in range(4):
            out_ref[8 * x + block] = high


def high_copies(summed, resid):
    return pl.pallas_call(
        high_kernel,
        in_specs=[VMEM, VMEM],
        out_specs=VMEM,
        out_shape=jax.ShapeDtypeStruct((32, 32, 512), BF),
        name="high_copies",
    )(summed, resid)


def term_kernel(half_ref, p0, p1, p2, p3, high_ref, rows_ref, out_ref):
    half = half_ref[0]
    for i in range(2):
        weights = [rows_ref[i, :, half, :, piece].reshape(256, 512) for piece in range(3)]
        for group, pair_ref in enumerate((p0, p1, p2, p3)):
            total = dot(pair_ref[0:256], weights[0], NT)
            total += dot(pair_ref[256:512], weights[1], NT)
            total += dot(high_ref[lax.rem(half_ref[1] + (4 - group), 4)], weights[2], NT)
            total = total.astype(BF)
            for part in range(2):
                out_ref[2 * i + part, group * 256 : (group + 1) * 256, :] = total[
                    :, part * 128 : (part + 1) * 128
                ]


def term_half(half, pairs, high, rows):
    return pl.pallas_call(
        term_kernel,
        in_specs=[pl.BlockSpec(memory_space=pltpu.SMEM)] + [VMEM] * 6,
        out_specs=VMEM,
        out_shape=jax.ShapeDtypeStruct((4, 1024, 128), BF),
        compiler_params=pltpu.CompilerParams(vmem_limit_bytes=40 * 1024 * 1024),
        cost_estimate=pl.CostEstimate(
            flops=2 * 1024 * 1536 * 512, bytes_accessed=6 * 1024 * 1024, transcendentals=0
        ),
        name="term_half",
    )(half, *pairs, high, rows)


def spread_kernel(terms_ref, p0, p1, p2, p3, out_ref):
    total = terms_ref[0].astype(F32)
    for part in range(1, 4):
        total += terms_ref[part].astype(F32)
    joined = total.astype(BF)
    row = lax.broadcasted_iota(jnp.int32, (1024, 256), 0)
    for two in range(2):
        moved = None
        for odd, pair_ref in enumerate(((p0, p1), (p2, p3))[two]):
            group = 2 * two + odd
            shard = pair_ref[512:513, 0:256].astype(jnp.int32)
            rank = pair_ref[512:513, 256:512].astype(jnp.int32)
            slot = shard * 16 + (odd * 8 + rank)
            hot = jnp.where(row == slot, 1.0, 0.0).astype(BF)
            part = dot(hot, joined[group * 256 : (group + 1) * 256])
            moved = part if moved is None else moved + part
        out_ref[:, two * 16 : (two + 1) * 16, :] = moved.astype(BF).reshape(64, 16, 128)


def spread(terms, pairs):
    return pl.pallas_call(
        spread_kernel,
        in_specs=[VMEM] * 5,
        out_specs=VMEM,
        out_shape=jax.ShapeDtypeStruct((64, 32, 128), BF),
        compiler_params=pltpu.CompilerParams(vmem_limit_bytes=40 * 1024 * 1024),
        name="spread",
    )(terms, *pairs)


def source_rows(tile, x):
    tile = tile.astype(F32)
    order = [8 * ((x - group) % 4) for group in range(4)]
    return [tile[at : at + 8] for at in order]


def chain_kernel(rows_ref, goal_ref, left_ref, in_ref, out_ref, grad_ref, final_ref, h0, h1, h2):
    for block in range(8):
        tiles = [
            jnp.concatenate(
                source_rows(rows_ref[block, x], x) + source_rows(rows_ref[block, 4 + x], x), axis=0
            )
            for x in range(4)
        ]
        for k in range(4):
            lane = (k // 2) * 64
            x = 2 * (k % 2)
            h0[:, block * 512 + k * 128 : block * 512 + (k + 1) * 128] = jnp.concatenate(
                [tiles[x][:, lane : lane + 64], tiles[x + 1][:, lane : lane + 64]], axis=1
            )
    goal = goal_ref[...].astype(F32)
    left = left_ref[...].astype(F32)
    states = (h0, h1, h2)
    invs, pres = [], []
    for step in range(3):
        state = states[step][...]
        inv = lax.rsqrt(jnp.sum(state * state, axis=-1, keepdims=True) * (1.0 / 4096) + 1e-06)
        pre = dot((state * inv).astype(BF), in_ref[...])
        active = (pre * jax.nn.sigmoid(pre)).astype(BF)
        invs.append(inv)
        pres.append(pre)
        after = state + dot(active, out_ref[...])
        if step < 2:
            states[step + 1][...] = after
        else:
            final_ref[...] = after.astype(BF)
    for step in (2, 1, 0):
        inv, pre = invs[step], pres[step]
        live = jnp.where(left > step, pre - goal, 0.0)
        if step == 2:
            dpre = live.astype(BF)
        else:
            dact = dot(grad_ref[...].astype(BF), out_ref[...], NT)
            sig = jax.nn.sigmoid(pre)
            dpre = (dact * (sig + pre * sig * (1.0 - sig)) + live).astype(BF)
        dnorm = dot(dpre, in_ref[...], NT)
        state = states[step][...]
        mean = jnp.sum(dnorm * state, axis=-1, keepdims=True) * (1.0 / 4096)
        back = inv * dnorm - state * (inv * inv * inv * mean)
        if step < 2:
            back = grad_ref[...] + back
        grad_ref[...] = back


def chain(rows, goal, left, step_in, step_out):
    return pl.pallas_call(
        chain_kernel,
        in_specs=[VMEM] * 5,
        out_specs=[VMEM] * 2,
        out_shape=[
            jax.ShapeDtypeStruct((64, 4096), F32),
            jax.ShapeDtypeStruct((64, 4096), BF),
        ],
        scratch_shapes=[pltpu.VMEM((64, 4096), F32)] * 3,
        compiler_params=pltpu.CompilerParams(vmem_limit_bytes=40 * 1024 * 1024),
        name="chain",
    )(rows, goal, left, step_in, step_out)


def per_device(
    partials, resid, low, mid, joining, step_in, step_out, targets, lengths, loss_mask, dest
):
    tensor, dp, z = ("y", "c"), ("z", "x"), "z"
    me = lax.axis_index("y") * 2 + lax.axis_index("c")
    core, along = lax.axis_index("c"), lax.axis_index("x")

    rows = lax.all_gather(jnp.swapaxes(joining, 1, 2), z).reshape(2, 2, 2, 2, 3, 64, 512)
    summed = lax.psum_scatter(partials, tensor, scatter_dimension=0, tiled=True)

    shard = dest[:, 0]
    earlier = jnp.arange(256)[:, None] > jnp.arange(256)[None, :]
    rank = jnp.sum(((shard[:, None] == shard[None, :]) & earlier).astype(jnp.int32), axis=1)
    extra = jnp.concatenate([shard, rank]).astype(BF)[None, :]
    extra = jnp.pad(extra, ((0, 15), (0, 0)))
    pair = jnp.concatenate([low, mid, extra], axis=0)
    pairs = [pair] + [lax.ppermute(pair, "x", ring(4, shift)) for shift in range(1, 4)]

    left = remaining_steps(lengths[0], loss_mask, 256).astype(BF)
    side = lax.dynamic_slice_in_dim(targets, me * 16, 16, 1)
    side = jnp.concatenate([side, jnp.broadcast_to(left[:, None], (256, 16))], axis=1)
    slot = jnp.arange(512, dtype=jnp.int32)[:, None] == (shard * 8 + rank)[None, :]
    side = jnp.dot(slot.astype(BF), side, preferred_element_type=F32).astype(BF)
    side = lax.all_to_all(side.reshape(64, 2, 128), dp, split_axis=0, concat_axis=0, tiled=True)

    resid, side = lax.optimization_barrier((resid, side))
    resid = lax.all_to_all(
        resid.reshape(8, 32, 512), tensor, split_axis=0, concat_axis=0, tiled=True
    )
    high = high_copies(summed, resid)
    high, side, *pairs = lax.optimization_barrier((high, side, *pairs))
    high = lax.all_to_all(high, ("x",) + tensor, split_axis=0, concat_axis=0, tiled=True)
    high, side = lax.optimization_barrier((high, side))
    side = lax.all_to_all(
        side.reshape(8, 16, 128), tensor, split_axis=0, concat_axis=0, tiled=True
    )
    high, side = lax.optimization_barrier((high, side))
    side = side.reshape(8, 64, 32)
    goal = jnp.swapaxes(side[:, :, :16], 0, 1).reshape(64, 128)
    left = jnp.broadcast_to(side[0, :, 16:17], (64, 128))
    high = high.reshape(4, 256, 512)

    other = term_half(jnp.stack([1 - core, along]).astype(jnp.int32), pairs, high, rows)
    other = lax.ppermute(other, "c", ring(2, 1))
    own = term_half(jnp.stack([core, along]).astype(jnp.int32), pairs, high, rows)
    terms = (own.astype(F32) + other.astype(F32)).astype(BF)
    terms = lax.all_to_all(terms, "y", split_axis=0, concat_axis=0, tiled=True)
    moved = spread(terms, pairs)
    moved = lax.all_to_all(moved, dp, split_axis=0, concat_axis=0, tiled=True)
    moved = lax.all_to_all(
        moved.reshape(8, 256, 128), tensor, split_axis=0, concat_axis=0, tiled=True
    )
    grad, final = chain(moved.reshape(8, 8, 32, 128), goal, left, step_in, step_out)
    return (grad, final)


def ring(size, shift):
    return [(i, (i + shift) % size) for i in range(size)]


def solution(mesh):
    fine = Mesh(mesh.devices.reshape(16, 4, 4, 2), ("z", "x", "y", "c"))
    dp, tensor = ("z", "x"), ("y", "c")
    in_specs = (
        P(dp, tensor),
        P(dp, tensor),
        P(dp, tensor),
        P(dp, tensor),
        P(None, tensor, dp),
        P(),
        P(),
        P(dp, None),
        P(dp, None),
        P(dp),
        P(dp, None),
    )
    out_specs = (P(dp + tensor, None), P(dp + tensor, None))
    return jax.shard_map(
        per_device, mesh=fine, in_specs=in_specs, out_specs=out_specs, check_vma=False
    )
```

```python
import jax
import jax.numpy as jnp
from jax import lax
from jax.experimental import pallas as pl
from jax.experimental.pallas import tpu as pltpu
from jax.sharding import Mesh, PartitionSpec as P

BF = jnp.bfloat16
F32 = jnp.float32
NT = (((1,), (1,)), ((), ()))
NN = (((1,), (0,)), ((), ()))
VMEM = pl.BlockSpec(memory_space=pltpu.VMEM)


def dot(a, b, dims=NN):
    return lax.dot_general(a, b, dims, preferred_element_type=F32)


def remaining_steps(sizes, mask, count):
    ends = jnp.cumsum(sizes)
    starts = ends - sizes
    place = jnp.arange(count, dtype=jnp.int32)[:, None]
    inside = (place >= starts[None, :]) & (place < ends[None, :])
    offset = jnp.sum(jnp.where(inside, place - starts[None, :], 0), axis=1)
    length = jnp.sum(jnp.where(inside, sizes[None, :], 0), axis=1)
    return (jnp.minimum(length - 1 - offset, 3) * mask).astype(F32)


def high_kernel(summed_ref, resid_ref, out_ref):
    for block in range(8):
        total = summed_ref[:, block * 512 : (block + 1) * 512].astype(F32)
        high = (total + resid_ref[block].astype(F32)).astype(BF)
        for x in range(4):
            out_ref[8 * x + block] = high


def high_copies(summed, resid):
    return pl.pallas_call(
        high_kernel,
        in_specs=[VMEM, VMEM],
        out_specs=VMEM,
        out_shape=jax.ShapeDtypeStruct((32, 32, 512), BF),
        name="high_copies",
    )(summed, resid)


def term_kernel(half_ref, p0, p1, p2, p3, high_ref, rows_ref, out_ref):
    half = half_ref[0]
    for i in range(2):
        weights = [rows_ref[i, :, half, :, piece].reshape(256, 512) for piece in range(3)]
        for group, pair_ref in enumerate((p0, p1, p2, p3)):
            total = dot(pair_ref[0:256], weights[0], NT)
            total += dot(pair_ref[256:512], weights[1], NT)
            total += dot(high_ref[lax.rem(half_ref[1] + (4 - group), 4)], weights[2], NT)
            total = total.astype(BF)
            for part in range(2):
                out_ref[2 * i + part, group * 256 : (group + 1) * 256, :] = total[
                    :, part * 128 : (part + 1) * 128
                ]


def term_half(half, pairs, high, rows):
    return pl.pallas_call(
        term_kernel,
        in_specs=[pl.BlockSpec(memory_space=pltpu.SMEM)] + [VMEM] * 6,
        out_specs=VMEM,
        out_shape=jax.ShapeDtypeStruct((4, 1024, 128), BF),
        compiler_params=pltpu.CompilerParams(vmem_limit_bytes=40 * 1024 * 1024),
        cost_estimate=pl.CostEstimate(
            flops=2 * 1024 * 1536 * 512, bytes_accessed=6 * 1024 * 1024, transcendentals=0
        ),
        name="term_half",
    )(half, *pairs, high, rows)


def spread_kernel(terms_ref, p0, p1, p2, p3, out_ref):
    total = terms_ref[0].astype(F32)
    for part in range(1, 4):
        total += terms_ref[part].astype(F32)
    joined = total.astype(BF)
    row = lax.broadcasted_iota(jnp.int32, (1024, 256), 0)
    for two in range(2):
        moved = None
        for odd, pair_ref in enumerate(((p0, p1), (p2, p3))[two]):
            group = 2 * two + odd
            shard = pair_ref[512:513, 0:256].astype(jnp.int32)
            rank = pair_ref[512:513, 256:512].astype(jnp.int32)
            slot = shard * 16 + (odd * 8 + rank)
            hot = jnp.where(row == slot, 1.0, 0.0).astype(BF)
            part = dot(hot, joined[group * 256 : (group + 1) * 256])
            moved = part if moved is None else moved + part
        out_ref[:, two * 16 : (two + 1) * 16, :] = moved.astype(BF).reshape(64, 16, 128)


def spread(terms, pairs):
    return pl.pallas_call(
        spread_kernel,
        in_specs=[VMEM] * 5,
        out_specs=VMEM,
        out_shape=jax.ShapeDtypeStruct((64, 32, 128), BF),
        compiler_params=pltpu.CompilerParams(vmem_limit_bytes=40 * 1024 * 1024),
        name="spread",
    )(terms, *pairs)


def source_rows(tile, x):
    tile = tile.astype(F32)
    order = [8 * ((x - group) % 4) for group in range(4)]
    return [tile[at : at + 8] for at in order]


def chain_kernel(rows_ref, goal_ref, left_ref, in_ref, out_ref, grad_ref, final_ref, h0, h1, h2):
    for block in range(8):
        tiles = [
            jnp.concatenate(
                source_rows(rows_ref[block, x], x) + source_rows(rows_ref[block, 4 + x], x), axis=0
            )
            for x in range(4)
        ]
        for k in range(4):
            lane = (k // 2) * 64
            x = 2 * (k % 2)
            h0[:, block * 512 + k * 128 : block * 512 + (k + 1) * 128] = jnp.concatenate(
                [tiles[x][:, lane : lane + 64], tiles[x + 1][:, lane : lane + 64]], axis=1
            )
    goal = goal_ref[...].astype(F32)
    left = left_ref[...].astype(F32)
    states = (h0, h1, h2)
    invs, pres = [], []
    for step in range(3):
        state = states[step][...]
        inv = lax.rsqrt(jnp.sum(state * state, axis=-1, keepdims=True) * (1.0 / 4096) + 1e-06)
        pre = dot((state * inv).astype(BF), in_ref[...])
        active = (pre * jax.nn.sigmoid(pre)).astype(BF)
        invs.append(inv)
        pres.append(pre)
        after = state + dot(active, out_ref[...])
        if step < 2:
            states[step + 1][...] = after
        else:
            final_ref[...] = after.astype(BF)
    for step in (2, 1, 0):
        inv, pre = invs[step], pres[step]
        live = jnp.where(left > step, pre - goal, 0.0)
        if step == 2:
            dpre = live.astype(BF)
        else:
            dact = dot(grad_ref[...].astype(BF), out_ref[...], NT)
            sig = jax.nn.sigmoid(pre)
            dpre = (dact * (sig + pre * sig * (1.0 - sig)) + live).astype(BF)
        dnorm = dot(dpre, in_ref[...], NT)
        state = states[step][...]
        mean = jnp.sum(dnorm * state, axis=-1, keepdims=True) * (1.0 / 4096)
        back = inv * dnorm - state * (inv * inv * inv * mean)
        if step < 2:
            back = grad_ref[...] + back
        grad_ref[...] = back


def chain(rows, goal, left, step_in, step_out):
    return pl.pallas_call(
        chain_kernel,
        in_specs=[VMEM] * 5,
        out_specs=[VMEM] * 2,
        out_shape=[
            jax.ShapeDtypeStruct((64, 4096), F32),
            jax.ShapeDtypeStruct((64, 4096), BF),
        ],
        scratch_shapes=[pltpu.VMEM((64, 4096), F32)] * 3,
        compiler_params=pltpu.CompilerParams(vmem_limit_bytes=40 * 1024 * 1024),
        name="chain",
    )(rows, goal, left, step_in, step_out)


def per_device(
    partials, resid, low, mid, joining, step_in, step_out, targets, lengths, loss_mask, dest
):
    tensor, dp, z = ("y", "c"), ("z", "x"), "z"
    me = lax.axis_index("y") * 2 + lax.axis_index("c")
    core, along = lax.axis_index("c"), lax.axis_index("x")

    rows = lax.all_gather(jnp.swapaxes(joining, 1, 2), z).reshape(2, 2, 2, 2, 3, 64, 512)
    summed = lax.psum_scatter(partials, tensor, scatter_dimension=0, tiled=True)

    shard = dest[:, 0]
    earlier = jnp.arange(256)[:, None] > jnp.arange(256)[None, :]
    rank = jnp.sum(((shard[:, None] == shard[None, :]) & earlier).astype(jnp.int32), axis=1)
    extra = jnp.concatenate([shard, rank]).astype(BF)[None, :]
    extra = jnp.pad(extra, ((0, 15), (0, 0)))
    pair = jnp.concatenate([low, mid, extra], axis=0)
    pairs = [pair] + [lax.ppermute(pair, "x", ring(4, shift)) for shift in range(1, 4)]

    left = remaining_steps(lengths[0], loss_mask, 256).astype(BF)
    side = lax.dynamic_slice_in_dim(targets, me * 16, 16, 1)
    side = jnp.concatenate([side, jnp.broadcast_to(left[:, None], (256, 16))], axis=1)
    slot = jnp.arange(512, dtype=jnp.int32)[:, None] == (shard * 8 + rank)[None, :]
    side = jnp.dot(slot.astype(BF), side, preferred_element_type=F32).astype(BF)
    side = lax.all_to_all(side.reshape(64, 2, 128), dp, split_axis=0, concat_axis=0, tiled=True)

    side = jnp.concatenate([resid.reshape(8, 32, 512), side.reshape(8, 4, 512)], axis=1)
    side = lax.all_to_all(side, tensor, split_axis=0, concat_axis=0, tiled=True)
    resid, side = side[:, :32], side[:, 32:].reshape(8, 64, 32)
    goal = jnp.swapaxes(side[:, :, :16], 0, 1).reshape(64, 128)
    left = jnp.broadcast_to(side[0, :, 16:17], (64, 128))

    high = high_copies(summed, resid)
    high, *pairs = lax.optimization_barrier((high, *pairs))
    high = lax.all_to_all(high, ("x",) + tensor, split_axis=0, concat_axis=0, tiled=True)
    high = high.reshape(4, 256, 512)

    other = term_half(jnp.stack([1 - core, along]).astype(jnp.int32), pairs, high, rows)
    other = lax.ppermute(other, "c", ring(2, 1))
    own = term_half(jnp.stack([core, along]).astype(jnp.int32), pairs, high, rows)
    terms = (own.astype(F32) + other.astype(F32)).astype(BF)
    terms = lax.all_to_all(terms, "y", split_axis=0, concat_axis=0, tiled=True)
    moved = spread(terms, pairs)
    moved = lax.all_to_all(moved, dp, split_axis=0, concat_axis=0, tiled=True)
    moved = lax.all_to_all(
        moved.reshape(8, 256, 128), tensor, split_axis=0, concat_axis=0, tiled=True
    )
    grad, final = chain(moved.reshape(8, 8, 32, 128), goal, left, step_in, step_out)
    return (grad, final)


def ring(size, shift):
    return [(i, (i + shift) % size) for i in range(size)]


def solution(mesh):
    fine = Mesh(mesh.devices.reshape(16, 4, 4, 2), ("z", "x", "y", "c"))
    dp, tensor = ("z", "x"), ("y", "c")
    in_specs = (
        P(dp, tensor),
        P(dp, tensor),
        P(dp, tensor),
        P(dp, tensor),
        P(None, tensor, dp),
        P(),
        P(),
        P(dp, None),
        P(dp, None),
        P(dp),
        P(dp, None),
    )
    out_specs = (P(dp + tensor, None), P(dp + tensor, None))
    return jax.shard_map(
        per_device, mesh=fine, in_specs=in_specs, out_specs=out_specs, check_vma=False
    )
```

```python
import jax
import jax.numpy as jnp
from jax import lax
from jax.experimental import pallas as pl
from jax.experimental.pallas import tpu as pltpu
from jax.sharding import Mesh, PartitionSpec as P

BF = jnp.bfloat16
F32 = jnp.float32
NT = (((1,), (1,)), ((), ()))
NN = (((1,), (0,)), ((), ()))
VMEM = pl.BlockSpec(memory_space=pltpu.VMEM)


def dot(a, b, dims=NN):
    return lax.dot_general(a, b, dims, preferred_element_type=F32)


def remaining_steps(sizes, mask, count):
    ends = jnp.cumsum(sizes)
    starts = ends - sizes
    place = jnp.arange(count, dtype=jnp.int32)[:, None]
    inside = (place >= starts[None, :]) & (place < ends[None, :])
    offset = jnp.sum(jnp.where(inside, place - starts[None, :], 0), axis=1)
    length = jnp.sum(jnp.where(inside, sizes[None, :], 0), axis=1)
    return (jnp.minimum(length - 1 - offset, 3) * mask).astype(F32)


def high_kernel(summed_ref, resid_ref, out_ref):
    for block in range(8):
        total = summed_ref[:, block * 512 : (block + 1) * 512].astype(F32)
        high = (total + resid_ref[block].astype(F32)).astype(BF)
        for x in range(4):
            out_ref[8 * x + block] = high


def high_copies(summed, resid):
    return pl.pallas_call(
        high_kernel,
        in_specs=[VMEM, VMEM],
        out_specs=VMEM,
        out_shape=jax.ShapeDtypeStruct((32, 32, 512), BF),
        name="high_copies",
    )(summed, resid)


def term_kernel(half_ref, p0, p1, p2, p3, high_ref, rows_ref, out_ref):
    half = half_ref[0]
    for i in range(2):
        weights = [rows_ref[i, :, half, :, piece].reshape(256, 512) for piece in range(3)]
        for group, pair_ref in enumerate((p0, p1, p2, p3)):
            total = dot(pair_ref[0:256], weights[0], NT)
            total += dot(pair_ref[256:512], weights[1], NT)
            total += dot(high_ref[lax.rem(half_ref[1] + (4 - group), 4)], weights[2], NT)
            total = total.astype(BF)
            for part in range(2):
                out_ref[2 * i + part, group * 256 : (group + 1) * 256, :] = total[
                    :, part * 128 : (part + 1) * 128
                ]


def term_half(half, pairs, high, rows):
    return pl.pallas_call(
        term_kernel,
        in_specs=[pl.BlockSpec(memory_space=pltpu.SMEM)] + [VMEM] * 6,
        out_specs=VMEM,
        out_shape=jax.ShapeDtypeStruct((4, 1024, 128), BF),
        compiler_params=pltpu.CompilerParams(vmem_limit_bytes=40 * 1024 * 1024),
        cost_estimate=pl.CostEstimate(
            flops=2 * 1024 * 1536 * 512, bytes_accessed=6 * 1024 * 1024, transcendentals=0
        ),
        name="term_half",
    )(half, *pairs, high, rows)


def spread_kernel(terms_ref, p0, p1, p2, p3, out_ref):
    total = terms_ref[0].astype(F32)
    for part in range(1, 4):
        total += terms_ref[part].astype(F32)
    joined = total.astype(BF)
    row = lax.broadcasted_iota(jnp.int32, (1024, 256), 0)
    for two in range(2):
        moved = None
        for odd, pair_ref in enumerate(((p0, p1), (p2, p3))[two]):
            group = 2 * two + odd
            shard = pair_ref[512:513, 0:256].astype(jnp.int32)
            rank = pair_ref[512:513, 256:512].astype(jnp.int32)
            slot = shard * 16 + (odd * 8 + rank)
            hot = jnp.where(row == slot, 1.0, 0.0).astype(BF)
            part = dot(hot, joined[group * 256 : (group + 1) * 256])
            moved = part if moved is None else moved + part
        out_ref[:, two * 16 : (two + 1) * 16, :] = moved.astype(BF).reshape(64, 16, 128)


def spread(terms, pairs):
    return pl.pallas_call(
        spread_kernel,
        in_specs=[VMEM] * 5,
        out_specs=VMEM,
        out_shape=jax.ShapeDtypeStruct((64, 32, 128), BF),
        compiler_params=pltpu.CompilerParams(vmem_limit_bytes=40 * 1024 * 1024),
        name="spread",
    )(terms, *pairs)


def source_rows(tile, x):
    tile = tile.astype(F32)
    order = [8 * ((x - group) % 4) for group in range(4)]
    return [tile[at : at + 8] for at in order]


def chain_kernel(rows_ref, goal_ref, left_ref, in_ref, out_ref, grad_ref, final_ref, h0, h1, h2):
    for block in range(8):
        tiles = [
            jnp.concatenate(
                source_rows(rows_ref[block, x], x) + source_rows(rows_ref[block, 4 + x], x), axis=0
            )
            for x in range(4)
        ]
        for k in range(4):
            lane = (k // 2) * 64
            x = 2 * (k % 2)
            h0[:, block * 512 + k * 128 : block * 512 + (k + 1) * 128] = jnp.concatenate(
                [tiles[x][:, lane : lane + 64], tiles[x + 1][:, lane : lane + 64]], axis=1
            )
    goal = goal_ref[...].astype(F32)
    left = left_ref[...].astype(F32)
    states = (h0, h1, h2)
    invs, pres = [], []
    for step in range(3):
        state = states[step][...]
        inv = lax.rsqrt(jnp.sum(state * state, axis=-1, keepdims=True) * (1.0 / 4096) + 1e-06)
        pre = inv * dot(state.astype(BF), in_ref[...])
        active = (pre * jax.nn.sigmoid(pre)).astype(BF)
        invs.append(inv)
        pres.append(pre)
        after = state + dot(active, out_ref[...])
        if step < 2:
            states[step + 1][...] = after
        else:
            final_ref[...] = after.astype(BF)
    for step in (2, 1, 0):
        inv, pre = invs[step], pres[step]
        live = jnp.where(left > step, pre - goal, 0.0)
        if step == 2:
            dpre = live
        else:
            dact = dot(grad_ref[...].astype(BF), out_ref[...], NT)
            sig = jax.nn.sigmoid(pre)
            dpre = dact * (sig + pre * sig * (1.0 - sig)) + live
        mean = jnp.sum(dpre * pre, axis=-1, keepdims=True) * (1.0 / 4096)
        back = dot((inv * dpre).astype(BF), in_ref[...], NT) - states[step][...] * (inv * inv * mean)
        if step < 2:
            back = grad_ref[...] + back
        grad_ref[...] = back


def chain(rows, goal, left, step_in, step_out):
    return pl.pallas_call(
        chain_kernel,
        in_specs=[VMEM] * 5,
        out_specs=[VMEM] * 2,
        out_shape=[
            jax.ShapeDtypeStruct((64, 4096), F32),
            jax.ShapeDtypeStruct((64, 4096), BF),
        ],
        scratch_shapes=[pltpu.VMEM((64, 4096), F32)] * 3,
        compiler_params=pltpu.CompilerParams(vmem_limit_bytes=40 * 1024 * 1024),
        name="chain",
    )(rows, goal, left, step_in, step_out)


def per_device(
    partials, resid, low, mid, joining, step_in, step_out, targets, lengths, loss_mask, dest
):
    tensor, dp, z = ("y", "c"), ("z", "x"), "z"
    me = lax.axis_index("y") * 2 + lax.axis_index("c")
    core, along = lax.axis_index("c"), lax.axis_index("x")

    rows = lax.all_gather(jnp.swapaxes(joining, 1, 2), z).reshape(2, 2, 2, 2, 3, 64, 512)
    summed = lax.psum_scatter(partials, tensor, scatter_dimension=0, tiled=True)

    shard = dest[:, 0]
    earlier = jnp.arange(256)[:, None] > jnp.arange(256)[None, :]
    rank = jnp.sum(((shard[:, None] == shard[None, :]) & earlier).astype(jnp.int32), axis=1)
    extra = jnp.concatenate([shard, rank]).astype(BF)[None, :]
    extra = jnp.pad(extra, ((0, 15), (0, 0)))
    pair = jnp.concatenate([low, mid, extra], axis=0)
    pairs = [pair] + [lax.ppermute(pair, "x", ring(4, shift)) for shift in range(1, 4)]

    left = remaining_steps(lengths[0], loss_mask, 256).astype(BF)
    side = lax.dynamic_slice_in_dim(targets, me * 16, 16, 1)
    side = jnp.concatenate([side, jnp.broadcast_to(left[:, None], (256, 16))], axis=1)
    slot = jnp.arange(512, dtype=jnp.int32)[:, None] == (shard * 8 + rank)[None, :]
    side = jnp.dot(slot.astype(BF), side, preferred_element_type=F32).astype(BF)
    side = lax.all_to_all(side.reshape(64, 2, 128), dp, split_axis=0, concat_axis=0, tiled=True)

    side = jnp.concatenate([resid.reshape(8, 32, 512), side.reshape(8, 4, 512)], axis=1)
    side = lax.all_to_all(side, tensor, split_axis=0, concat_axis=0, tiled=True)
    resid, side = side[:, :32], side[:, 32:].reshape(8, 64, 32)
    goal = jnp.swapaxes(side[:, :, :16], 0, 1).reshape(64, 128)
    left = jnp.broadcast_to(side[0, :, 16:17], (64, 128))

    high = high_copies(summed, resid)
    high, *pairs = lax.optimization_barrier((high, *pairs))
    high = lax.all_to_all(high, ("x",) + tensor, split_axis=0, concat_axis=0, tiled=True)
    high = high.reshape(4, 256, 512)

    other = term_half(jnp.stack([1 - core, along]).astype(jnp.int32), pairs, high, rows)
    other = lax.ppermute(other, "c", ring(2, 1))
    own = term_half(jnp.stack([core, along]).astype(jnp.int32), pairs, high, rows)
    terms = (own.astype(F32) + other.astype(F32)).astype(BF)
    terms = lax.all_to_all(terms, "y", split_axis=0, concat_axis=0, tiled=True)
    moved = spread(terms, pairs)
    moved = lax.all_to_all(moved, dp, split_axis=0, concat_axis=0, tiled=True)
    moved = lax.all_to_all(
        moved.reshape(8, 256, 128), tensor, split_axis=0, concat_axis=0, tiled=True
    )
    grad, final = chain(moved.reshape(8, 8, 32, 128), goal, left, step_in, step_out)
    return (grad, final)


def ring(size, shift):
    return [(i, (i + shift) % size) for i in range(size)]


def solution(mesh):
    fine = Mesh(mesh.devices.reshape(16, 4, 4, 2), ("z", "x", "y", "c"))
    dp, tensor = ("z", "x"), ("y", "c")
    in_specs = (
        P(dp, tensor),
        P(dp, tensor),
        P(dp, tensor),
        P(dp, tensor),
        P(None, tensor, dp),
        P(),
        P(),
        P(dp, None),
        P(dp, None),
        P(dp),
        P(dp, None),
    )
    out_specs = (P(dp + tensor, None), P(dp + tensor, None))
    return jax.shard_map(
        per_device, mesh=fine, in_specs=in_specs, out_specs=out_specs, check_vma=False
    )
```

```python
import jax
import jax.numpy as jnp
from jax import lax
from jax.experimental import pallas as pl
from jax.experimental.pallas import tpu as pltpu
from jax.sharding import Mesh, PartitionSpec as P

BF = jnp.bfloat16
F32 = jnp.float32
NT = (((1,), (1,)), ((), ()))
NN = (((1,), (0,)), ((), ()))
VMEM = pl.BlockSpec(memory_space=pltpu.VMEM)


def dot(a, b, dims=NN):
    return lax.dot_general(a, b, dims, preferred_element_type=F32)


def remaining_steps(sizes, mask, count):
    ends = jnp.cumsum(sizes)
    starts = ends - sizes
    place = jnp.arange(count, dtype=jnp.int32)[:, None]
    inside = (place >= starts[None, :]) & (place < ends[None, :])
    offset = jnp.sum(jnp.where(inside, place - starts[None, :], 0), axis=1)
    length = jnp.sum(jnp.where(inside, sizes[None, :], 0), axis=1)
    return (jnp.minimum(length - 1 - offset, 3) * mask).astype(F32)


def high_kernel(summed_ref, resid_ref, out_ref):
    for block in range(8):
        total = summed_ref[:, block * 512 : (block + 1) * 512].astype(F32)
        high = (total + resid_ref[block].astype(F32)).astype(BF)
        for x in range(4):
            out_ref[8 * x + block] = high


def high_copies(summed, resid):
    return pl.pallas_call(
        high_kernel,
        in_specs=[VMEM, VMEM],
        out_specs=VMEM,
        out_shape=jax.ShapeDtypeStruct((32, 32, 512), BF),
        name="high_copies",
    )(summed, resid)


def term_kernel(half_ref, p0, p1, p2, p3, high_ref, rows_ref, out_ref):
    half = half_ref[0]
    for i in range(2):
        weights = [rows_ref[i, :, half, :, piece].reshape(256, 512) for piece in range(3)]
        for group, pair_ref in enumerate((p0, p1, p2, p3)):
            total = dot(pair_ref[0:256], weights[0], NT)
            total += dot(pair_ref[256:512], weights[1], NT)
            total += dot(high_ref[lax.rem(half_ref[1] + (4 - group), 4)], weights[2], NT)
            total = total.astype(BF)
            for part in range(2):
                out_ref[2 * i + part, group * 256 : (group + 1) * 256, :] = total[
                    :, part * 128 : (part + 1) * 128
                ]


def term_half(half, pairs, high, rows):
    return pl.pallas_call(
        term_kernel,
        in_specs=[pl.BlockSpec(memory_space=pltpu.SMEM)] + [VMEM] * 6,
        out_specs=VMEM,
        out_shape=jax.ShapeDtypeStruct((4, 1024, 128), BF),
        compiler_params=pltpu.CompilerParams(vmem_limit_bytes=40 * 1024 * 1024),
        cost_estimate=pl.CostEstimate(
            flops=2 * 1024 * 1536 * 512, bytes_accessed=6 * 1024 * 1024, transcendentals=0
        ),
        name="term_half",
    )(half, *pairs, high, rows)


def spread_kernel(terms_ref, p0, p1, p2, p3, out_ref):
    total = terms_ref[0].astype(F32)
    for part in range(1, 4):
        total += terms_ref[part].astype(F32)
    joined = total.astype(BF)
    row = lax.broadcasted_iota(jnp.int32, (1024, 256), 0)
    for two in range(2):
        moved = None
        for odd, pair_ref in enumerate(((p0, p1), (p2, p3))[two]):
            group = 2 * two + odd
            extra = pair_ref[512:528].astype(F32)[0:1].astype(jnp.int32)
            shard, rank = extra[:, 0:256], extra[:, 256:512]
            slot = shard * 16 + (odd * 8 + rank)
            hot = jnp.where(row == slot, 1.0, 0.0).astype(BF)
            part = dot(hot, joined[group * 256 : (group + 1) * 256])
            moved = part if moved is None else moved + part
        out_ref[:, two * 16 : (two + 1) * 16, :] = moved.astype(BF).reshape(64, 16, 128)


def spread(terms, pairs):
    return pl.pallas_call(
        spread_kernel,
        in_specs=[VMEM] * 5,
        out_specs=VMEM,
        out_shape=jax.ShapeDtypeStruct((64, 32, 128), BF),
        compiler_params=pltpu.CompilerParams(vmem_limit_bytes=40 * 1024 * 1024),
        name="spread",
    )(terms, *pairs)


def source_rows(tile, x):
    tile = tile.astype(F32)
    order = [8 * ((x - group) % 4) for group in range(4)]
    return [tile[at : at + 8] for at in order]


def chain_kernel(rows_ref, goal_ref, left_ref, in_ref, out_ref, grad_ref, final_ref, h0, h1, h2):
    for block in range(8):
        tiles = [
            jnp.concatenate(
                source_rows(rows_ref[block, x], x) + source_rows(rows_ref[block, 4 + x], x), axis=0
            )
            for x in range(4)
        ]
        for k in range(4):
            lane = (k // 2) * 64
            x = 2 * (k % 2)
            h0[:, block * 512 + k * 128 : block * 512 + (k + 1) * 128] = jnp.concatenate(
                [tiles[x][:, lane : lane + 64], tiles[x + 1][:, lane : lane + 64]], axis=1
            )
    goal = goal_ref[...].astype(F32)
    left = left_ref[...].astype(F32)
    states = (h0, h1, h2)
    invs, pres = [], []
    for step in range(3):
        state = states[step][...]
        inv = lax.rsqrt(jnp.sum(state * state, axis=-1, keepdims=True) * (1.0 / 4096) + 1e-06)
        pre = inv * dot(state.astype(BF), in_ref[...])
        active = (pre * jax.nn.sigmoid(pre)).astype(BF)
        invs.append(inv)
        pres.append(pre)
        after = state + dot(active, out_ref[...])
        if step < 2:
            states[step + 1][...] = after
        else:
            final_ref[...] = after.astype(BF)
    for step in (2, 1, 0):
        inv, pre = invs[step], pres[step]
        live = jnp.where(left > step, pre - goal, 0.0)
        if step == 2:
            dpre = live
        else:
            dact = dot(grad_ref[...].astype(BF), out_ref[...], NT)
            sig = jax.nn.sigmoid(pre)
            dpre = dact * (sig + pre * sig * (1.0 - sig)) + live
        mean = jnp.sum(dpre * pre, axis=-1, keepdims=True) * (1.0 / 4096)
        back = dot((inv * dpre).astype(BF), in_ref[...], NT) - states[step][...] * (inv * inv * mean)
        if step < 2:
            back = grad_ref[...] + back
        grad_ref[...] = back


def chain(rows, goal, left, step_in, step_out):
    return pl.pallas_call(
        chain_kernel,
        in_specs=[VMEM] * 5,
        out_specs=[VMEM] * 2,
        out_shape=[
            jax.ShapeDtypeStruct((64, 4096), F32),
            jax.ShapeDtypeStruct((64, 4096), BF),
        ],
        scratch_shapes=[pltpu.VMEM((64, 4096), F32)] * 3,
        compiler_params=pltpu.CompilerParams(vmem_limit_bytes=40 * 1024 * 1024),
        name="chain",
    )(rows, goal, left, step_in, step_out)


def per_device(
    partials, resid, low, mid, joining, step_in, step_out, targets, lengths, loss_mask, dest
):
    tensor, dp, z = ("y", "c"), ("z", "x"), "z"
    me = lax.axis_index("y") * 2 + lax.axis_index("c")
    core, along = lax.axis_index("c"), lax.axis_index("x")

    rows = lax.all_gather(jnp.swapaxes(joining, 1, 2), z).reshape(2, 2, 2, 2, 3, 64, 512)
    summed = lax.psum_scatter(partials, tensor, scatter_dimension=0, tiled=True)

    shard = dest[:, 0]
    earlier = jnp.arange(256)[:, None] > jnp.arange(256)[None, :]
    rank = jnp.sum(((shard[:, None] == shard[None, :]) & earlier).astype(jnp.int32), axis=1)
    extra = jnp.concatenate([shard, rank]).astype(BF)[None, :]
    extra = jnp.pad(extra, ((0, 15), (0, 0)))
    pair = jnp.concatenate([low, mid, extra], axis=0)
    pairs = [pair] + [lax.ppermute(pair, "x", ring(4, shift)) for shift in range(1, 4)]

    left = remaining_steps(lengths[0], loss_mask, 256).astype(BF)
    side = lax.dynamic_slice_in_dim(targets, me * 16, 16, 1)
    side = jnp.concatenate([side, jnp.broadcast_to(left[:, None], (256, 16))], axis=1)
    slot = jnp.arange(512, dtype=jnp.int32)[:, None] == (shard * 8 + rank)[None, :]
    side = jnp.dot(slot.astype(BF), side, preferred_element_type=F32).astype(BF)
    side = lax.all_to_all(side.reshape(64, 2, 128), dp, split_axis=0, concat_axis=0, tiled=True)

    side = jnp.concatenate([resid.reshape(8, 32, 512), side.reshape(8, 4, 512)], axis=1)
    side = lax.all_to_all(side, tensor, split_axis=0, concat_axis=0, tiled=True)
    resid, side = side[:, :32], side[:, 32:].reshape(8, 64, 32)
    goal = jnp.swapaxes(side[:, :, :16], 0, 1).reshape(64, 128)
    left = jnp.broadcast_to(side[0, :, 16:17], (64, 128))

    high = high_copies(summed, resid)
    high, *pairs = lax.optimization_barrier((high, *pairs))
    high = lax.all_to_all(high, ("x",) + tensor, split_axis=0, concat_axis=0, tiled=True)
    high = high.reshape(4, 256, 512)

    other = term_half(jnp.stack([1 - core, along]).astype(jnp.int32), pairs, high, rows)
    other = lax.ppermute(other, "c", ring(2, 1))
    own = term_half(jnp.stack([core, along]).astype(jnp.int32), pairs, high, rows)
    terms = (own.astype(F32) + other.astype(F32)).astype(BF)
    terms = lax.all_to_all(terms, "y", split_axis=0, concat_axis=0, tiled=True)
    moved = spread(terms, pairs)
    moved = lax.all_to_all(moved, dp, split_axis=0, concat_axis=0, tiled=True)
    moved = lax.all_to_all(
        moved.reshape(8, 256, 128), tensor, split_axis=0, concat_axis=0, tiled=True
    )
    grad, final = chain(moved.reshape(8, 8, 32, 128), goal, left, step_in, step_out)
    return (grad, final)


def ring(size, shift):
    return [(i, (i + shift) % size) for i in range(size)]


def solution(mesh):
    fine = Mesh(mesh.devices.reshape(16, 4, 4, 2), ("z", "x", "y", "c"))
    dp, tensor = ("z", "x"), ("y", "c")
    in_specs = (
        P(dp, tensor),
        P(dp, tensor),
        P(dp, tensor),
        P(dp, tensor),
        P(None, tensor, dp),
        P(),
        P(),
        P(dp, None),
        P(dp, None),
        P(dp),
        P(dp, None),
    )
    out_specs = (P(dp + tensor, None), P(dp + tensor, None))
    return jax.shard_map(
        per_device, mesh=fine, in_specs=in_specs, out_specs=out_specs, check_vma=False
    )
```

```python
import jax
import jax.numpy as jnp
from jax import lax
from jax.experimental import pallas as pl
from jax.experimental.pallas import tpu as pltpu
from jax.sharding import Mesh, PartitionSpec as P

BF = jnp.bfloat16
F32 = jnp.float32
NT = (((1,), (1,)), ((), ()))
NN = (((1,), (0,)), ((), ()))
VMEM = pl.BlockSpec(memory_space=pltpu.VMEM)


def dot(a, b, dims=NN):
    return lax.dot_general(a, b, dims, preferred_element_type=F32)


def remaining_steps(sizes, mask, count):
    ends = jnp.cumsum(sizes)
    starts = ends - sizes
    place = jnp.arange(count, dtype=jnp.int32)[:, None]
    inside = (place >= starts[None, :]) & (place < ends[None, :])
    offset = jnp.sum(jnp.where(inside, place - starts[None, :], 0), axis=1)
    length = jnp.sum(jnp.where(inside, sizes[None, :], 0), axis=1)
    return (jnp.minimum(length - 1 - offset, 3) * mask).astype(F32)


def high_kernel(summed_ref, resid_ref, out_ref):
    for block in range(8):
        total = summed_ref[:, block * 512 : (block + 1) * 512].astype(F32)
        high = (total + resid_ref[block].astype(F32)).astype(BF)
        for x in range(4):
            out_ref[8 * x + block] = high


def high_copies(summed, resid):
    return pl.pallas_call(
        high_kernel,
        in_specs=[VMEM, VMEM],
        out_specs=VMEM,
        out_shape=jax.ShapeDtypeStruct((32, 32, 512), BF),
        name="high_copies",
    )(summed, resid)


def term_kernel(half_ref, p0, p1, p2, p3, high_ref, rows_ref, out_ref):
    half = half_ref[0]
    pairs = (p0, p1, p2, p3)
    lows = jnp.concatenate([pair_ref[0:256] for pair_ref in pairs], axis=0)
    mids = jnp.concatenate([pair_ref[256:512] for pair_ref in pairs], axis=0)
    highs = jnp.concatenate(
        [high_ref[lax.rem(half_ref[1] + (4 - group), 4)] for group in range(4)], axis=0
    )
    for i in range(2):
        weights = [rows_ref[i, :, half, :, piece].reshape(256, 512) for piece in range(3)]
        total = dot(lows, weights[0], NT)
        total += dot(mids, weights[1], NT)
        total += dot(highs, weights[2], NT)
        total = total.astype(BF)
        for part in range(2):
            out_ref[2 * i + part] = total[:, part * 128 : (part + 1) * 128]


def term_half(half, pairs, high, rows):
    return pl.pallas_call(
        term_kernel,
        in_specs=[pl.BlockSpec(memory_space=pltpu.SMEM)] + [VMEM] * 6,
        out_specs=VMEM,
        out_shape=jax.ShapeDtypeStruct((4, 1024, 128), BF),
        compiler_params=pltpu.CompilerParams(vmem_limit_bytes=40 * 1024 * 1024),
        cost_estimate=pl.CostEstimate(
            flops=2 * 1024 * 1536 * 512, bytes_accessed=6 * 1024 * 1024, transcendentals=0
        ),
        name="term_half",
    )(half, *pairs, high, rows)


def spread_kernel(terms_ref, p0, p1, p2, p3, out_ref):
    total = terms_ref[0].astype(F32)
    for part in range(1, 4):
        total += terms_ref[part].astype(F32)
    joined = total.astype(BF)
    row = lax.broadcasted_iota(jnp.int32, (1024, 256), 0)
    for two in range(2):
        moved = None
        for odd, pair_ref in enumerate(((p0, p1), (p2, p3))[two]):
            group = 2 * two + odd
            extra = pair_ref[512:528].astype(F32)[0:1].astype(jnp.int32)
            shard, rank = extra[:, 0:256], extra[:, 256:512]
            slot = shard * 16 + (odd * 8 + rank)
            hot = jnp.where(row == slot, 1.0, 0.0).astype(BF)
            part = dot(hot, joined[group * 256 : (group + 1) * 256])
            moved = part if moved is None else moved + part
        out_ref[:, two * 16 : (two + 1) * 16, :] = moved.astype(BF).reshape(64, 16, 128)


def spread(terms, pairs):
    return pl.pallas_call(
        spread_kernel,
        in_specs=[VMEM] * 5,
        out_specs=VMEM,
        out_shape=jax.ShapeDtypeStruct((64, 32, 128), BF),
        compiler_params=pltpu.CompilerParams(vmem_limit_bytes=40 * 1024 * 1024),
        name="spread",
    )(terms, *pairs)


def source_rows(tile, x):
    tile = tile.astype(F32)
    order = [8 * ((x - group) % 4) for group in range(4)]
    return [tile[at : at + 8] for at in order]


def chain_kernel(rows_ref, goal_ref, left_ref, in_ref, out_ref, grad_ref, final_ref, h0, h1, h2):
    for block in range(8):
        tiles = [
            jnp.concatenate(
                source_rows(rows_ref[block, x], x) + source_rows(rows_ref[block, 4 + x], x), axis=0
            )
            for x in range(4)
        ]
        for k in range(4):
            lane = (k // 2) * 64
            x = 2 * (k % 2)
            h0[:, block * 512 + k * 128 : block * 512 + (k + 1) * 128] = jnp.concatenate(
                [tiles[x][:, lane : lane + 64], tiles[x + 1][:, lane : lane + 64]], axis=1
            )
    goal = goal_ref[...].astype(F32)
    left = left_ref[...].astype(F32)
    states = (h0, h1, h2)
    invs, pres = [], []
    for step in range(3):
        state = states[step][...]
        inv = lax.rsqrt(jnp.sum(state * state, axis=-1, keepdims=True) * (1.0 / 4096) + 1e-06)
        pre = inv * dot(state.astype(BF), in_ref[...])
        active = (pre * jax.nn.sigmoid(pre)).astype(BF)
        invs.append(inv)
        pres.append(pre)
        after = state + dot(active, out_ref[...])
        if step < 2:
            states[step + 1][...] = after
        else:
            final_ref[...] = after.astype(BF)
    for step in (2, 1, 0):
        inv, pre = invs[step], pres[step]
        live = jnp.where(left > step, pre - goal, 0.0)
        if step == 2:
            dpre = live
        else:
            dact = dot(grad_ref[...].astype(BF), out_ref[...], NT)
            sig = jax.nn.sigmoid(pre)
            dpre = dact * (sig + pre * sig * (1.0 - sig)) + live
        mean = jnp.sum(dpre * pre, axis=-1, keepdims=True) * (1.0 / 4096)
        back = dot((inv * dpre).astype(BF), in_ref[...], NT) - states[step][...] * (inv * inv * mean)
        if step < 2:
            back = grad_ref[...] + back
        grad_ref[...] = back


def chain(rows, goal, left, step_in, step_out):
    return pl.pallas_call(
        chain_kernel,
        in_specs=[VMEM] * 5,
        out_specs=[VMEM] * 2,
        out_shape=[
            jax.ShapeDtypeStruct((64, 4096), F32),
            jax.ShapeDtypeStruct((64, 4096), BF),
        ],
        scratch_shapes=[pltpu.VMEM((64, 4096), F32)] * 3,
        compiler_params=pltpu.CompilerParams(vmem_limit_bytes=40 * 1024 * 1024),
        name="chain",
    )(rows, goal, left, step_in, step_out)


def per_device(
    partials, resid, low, mid, joining, step_in, step_out, targets, lengths, loss_mask, dest
):
    tensor, dp, z = ("y", "c"), ("z", "x"), "z"
    me = lax.axis_index("y") * 2 + lax.axis_index("c")
    core, along = lax.axis_index("c"), lax.axis_index("x")

    rows = lax.all_gather(jnp.swapaxes(joining, 1, 2), z).reshape(2, 2, 2, 2, 3, 64, 512)
    summed = lax.psum_scatter(partials, tensor, scatter_dimension=0, tiled=True)

    shard = dest[:, 0]
    earlier = jnp.arange(256)[:, None] > jnp.arange(256)[None, :]
    rank = jnp.sum(((shard[:, None] == shard[None, :]) & earlier).astype(jnp.int32), axis=1)
    extra = jnp.concatenate([shard, rank]).astype(BF)[None, :]
    extra = jnp.pad(extra, ((0, 15), (0, 0)))
    pair = jnp.concatenate([low, mid, extra], axis=0)
    pairs = [pair] + [lax.ppermute(pair, "x", ring(4, shift)) for shift in range(1, 4)]

    left = remaining_steps(lengths[0], loss_mask, 256).astype(BF)
    side = lax.dynamic_slice_in_dim(targets, me * 16, 16, 1)
    side = jnp.concatenate([side, jnp.broadcast_to(left[:, None], (256, 16))], axis=1)
    slot = jnp.arange(512, dtype=jnp.int32)[:, None] == (shard * 8 + rank)[None, :]
    side = jnp.dot(slot.astype(BF), side, preferred_element_type=F32).astype(BF)
    side = lax.all_to_all(side.reshape(64, 2, 128), dp, split_axis=0, concat_axis=0, tiled=True)

    side = jnp.concatenate([resid.reshape(8, 32, 512), side.reshape(8, 4, 512)], axis=1)
    side = lax.all_to_all(side, tensor, split_axis=0, concat_axis=0, tiled=True)
    resid, side = side[:, :32], side[:, 32:].reshape(8, 64, 32)
    goal = jnp.swapaxes(side[:, :, :16], 0, 1).reshape(64, 128)
    left = jnp.broadcast_to(side[0, :, 16:17], (64, 128))

    high = high_copies(summed, resid)
    high, *pairs = lax.optimization_barrier((high, *pairs))
    high = lax.all_to_all(high, ("x",) + tensor, split_axis=0, concat_axis=0, tiled=True)
    high = high.reshape(4, 256, 512)

    other = term_half(jnp.stack([1 - core, along]).astype(jnp.int32), pairs, high, rows)
    other = lax.ppermute(other, "c", ring(2, 1))
    own = term_half(jnp.stack([core, along]).astype(jnp.int32), pairs, high, rows)
    terms = (own.astype(F32) + other.astype(F32)).astype(BF)
    terms = lax.all_to_all(terms, "y", split_axis=0, concat_axis=0, tiled=True)
    moved = spread(terms, pairs)
    moved = lax.all_to_all(moved, dp, split_axis=0, concat_axis=0, tiled=True)
    moved = lax.all_to_all(
        moved.reshape(8, 256, 128), tensor, split_axis=0, concat_axis=0, tiled=True
    )
    grad, final = chain(moved.reshape(8, 8, 32, 128), goal, left, step_in, step_out)
    return (grad, final)


def ring(size, shift):
    return [(i, (i + shift) % size) for i in range(size)]


def solution(mesh):
    fine = Mesh(mesh.devices.reshape(16, 4, 4, 2), ("z", "x", "y", "c"))
    dp, tensor = ("z", "x"), ("y", "c")
    in_specs = (
        P(dp, tensor),
        P(dp, tensor),
        P(dp, tensor),
        P(dp, tensor),
        P(None, tensor, dp),
        P(),
        P(),
        P(dp, None),
        P(dp, None),
        P(dp),
        P(dp, None),
    )
    out_specs = (P(dp + tensor, None), P(dp + tensor, None))
    return jax.shard_map(
        per_device, mesh=fine, in_specs=in_specs, out_specs=out_specs, check_vma=False
    )
```
